512 devices in a mesh: grp: 4 (over x), comp: 32 (over y, z_lo, core), tp: 4 (over z_hi).
Axes of the slice: x: 4, y: 8, z: 8 (z_hi: 4, z_lo: 2; z = z_hi * 2 + z_lo), core: 2. Of those that a mesh axis runs over, the one named last changes fastest.
Arguments:
- queries: bfloat16 [65536, 2560], P(('grp', 'comp'), 'tp'), parts along dimension 0, may hold values from -7 to 7
- comp_keys: bfloat16 [65536, 512], P(('grp', 'comp'), 'tp'), parts along dimension 0, may hold values from -4 to 4
- comp_values: bfloat16 [65536, 512], P(('grp', 'comp'), 'tp'), parts along dimension 0, may hold values from -4 to 4
- out_grad: bfloat16 [65536, 2560], P(('grp', 'comp'), 'tp'), parts along dimension 0, may hold values from -24 to 24
- prompt_keys: bfloat16 [4096, 512], P(('grp', 'comp'), 'tp'), parts along dimension 0, may hold values from -4 to 4
- prompt_values: bfloat16 [4096, 512], P(('grp', 'comp'), 'tp'), parts along dimension 0, may hold values from -4 to 4
- lengths: int32 [128], P(('grp', 'comp')), parts along dimension 0, may hold values from 1 to 4, as said below
Outputs:
- grad_queries: float32 [65536, 2560], P(('grp', 'comp'), 'tp'), parts along dimension 0
- grad_prompt_keys: float32 [4096, 512], P(('grp', 'comp'), 'tp'), parts along dimension 0
- grad_prompt_values: float32 [4096, 512], P(('grp', 'comp'), 'tp'), parts along dimension 0
- grad_comp_keys: float32 [65536, 512], P(('grp', 'comp'), 'tp'), parts along dimension 0
- grad_comp_values: float32 [65536, 512], P(('grp', 'comp'), 'tp'), parts along dimension 0
The draws below stay inside these ranges and needn't reach their ends.
There are 4 independent parts, one for each index of `grp`. The reference program is written for one: setup_inputs(seed, part) draws one part's arguments, and reference() takes and returns one part's arrays. A program takes and returns all parts, laid end to end along the dimension named above; each array names one. Nothing has to cross between parts.
Inputs may be any that keep to these rules, and one draw needn't show every extreme that they name: `lengths`: in every draw one completion has exactly 4 blocks.
All inputs are finite; a program needn't handle non-finite values.
Results may differ from the reference program's by a relative error of at most 0.011.
Values may be sent and summed in bfloat16 or wider, within the bound.
No kernel may reach another device: no remote copies, remote signals or barrier semaphores. Data moves between devices by JAX's collectives and lax.ppermute only.
A program may use at most 64 MiB of HBM per device.

```python
import jax
import jax.numpy as jnp
from jax import lax

QH = 20
KVH = 4
HD = 128
BLK = 128
MAXB = 4
GROUP = 5
MAXLEN = 512
COMPS = 32
TOK = 16384
PROMPT = 1024


def draw_queries(key, part):
    key = jax.random.fold_in(key, 21)
    values = 1.5 * jax.random.truncated_normal(key, -4.0, 4.0, (TOK, QH * HD), jnp.float32)
    return values.astype(jnp.bfloat16)


def draw_prompt_keys(key, part):
    key = jax.random.fold_in(key, 22)
    values = jax.random.truncated_normal(key, -4.0, 4.0, (PROMPT, KVH * HD), jnp.float32)
    return values.astype(jnp.bfloat16)


def draw_lengths(key, part):
    key = jax.random.fold_in(key, 23)
    first = jax.random.randint(jax.random.fold_in(key, 1), (COMPS,), 1, MAXB + 1)
    second = jax.random.randint(jax.random.fold_in(key, 2), (COMPS,), 1, MAXB + 1)
    blocks = jnp.minimum(first, second)
    longest = jax.random.randint(jax.random.fold_in(key, 3), (), 0, COMPS)
    places = jnp.arange(COMPS)
    blocks = jnp.where(places == longest, MAXB, blocks)
    return blocks.astype(jnp.int32)


def block_scale(rng, dims, shards, smallest, high):
    level, own = 1.0, jax.random.fold_in(rng, 6)
    for dim, parts in shards:
        steps = jnp.exp(jax.random.uniform(jax.random.fold_in(own, dim), (parts,), jnp.float32, smallest / len(shards), high / len(shards)))
        level = level * jnp.repeat(steps, dims[dim] // parts).reshape([-1 if axis == dim else 1 for axis in range(len(dims))])
    return level


def gaussian(key, shape, scale, reach, cuts=(), kind=jnp.bfloat16):
    drawn = scale * jax.random.normal(key, shape, jnp.float32)
    if cuts:
        drawn = drawn * block_scale(key, shape, cuts, -0.22, 0.18)
    return jnp.clip(drawn, -reach, reach).astype(kind)


def setup_inputs(seed: int = 0, part: int = 0) -> dict:
    arg_keys = jax.random.split(jax.random.key(seed), 8)
    own_keys = jax.random.split(jax.random.fold_in(arg_keys[7], part), 8)
    return {
        "queries": draw_queries(jax.random.fold_in(jax.random.fold_in(arg_keys[7], part), 71), part),
        "comp_keys": gaussian(own_keys[1], (TOK, KVH * HD), 1.0, 4.0, ((0, 32), (1, 4))),
        "comp_values": gaussian(own_keys[2], (TOK, KVH * HD), 1.0, 4.0, ((0, 32), (1, 4))),
        "out_grad": gaussian(own_keys[3], (TOK, QH * HD), 4.0, 24.0, ((0, 32), (1, 4))),
        "prompt_keys": draw_prompt_keys(jax.random.fold_in(jax.random.fold_in(arg_keys[7], part), 71), part),
        "prompt_values": gaussian(own_keys[5], (PROMPT, KVH * HD), 1.0, 4.0, ((0, 32), (1, 4))),
        "lengths": draw_lengths(jax.random.fold_in(jax.random.fold_in(arg_keys[7], part), 71), part),
    }


def group_pass(items):
    query_group, grad_group, key_prompt, value_prompt, key_own, value_own = items
    softmax_scale = HD ** -0.5
    causal = jnp.arange(MAXLEN)[:, None] >= jnp.arange(MAXLEN)[None, :]
    key_blocks = key_own.reshape(COMPS, MAXLEN, HD).astype(jnp.float32)
    value_blocks = value_own.reshape(COMPS, MAXLEN, HD).astype(jnp.float32)
    prompt_kgrad = jnp.zeros((PROMPT, HD), jnp.float32)
    prompt_vgrad = jnp.zeros((PROMPT, HD), jnp.float32)
    own_kgrad = jnp.zeros((COMPS, MAXLEN, HD), jnp.float32)
    own_vgrad = jnp.zeros((COMPS, MAXLEN, HD), jnp.float32)
    query_grads = []
    for member in range(GROUP):
        query_head = query_group[member]
        grad_head = grad_group[member]
        query_blocks = query_head.reshape(COMPS, MAXLEN, HD).astype(jnp.float32)
        grad_blocks = grad_head.reshape(COMPS, MAXLEN, HD).astype(jnp.float32)
        prompt_scores = jnp.dot(query_head, key_prompt.T, preferred_element_type=jnp.float32) * softmax_scale
        own_scores = jnp.einsum("cld,cmd->clm", query_blocks, key_blocks) * softmax_scale
        own_scores = jnp.where(causal[None], own_scores, -jnp.inf)
        row_max = jnp.maximum(jnp.max(prompt_scores, 1), jnp.max(own_scores, 2).reshape(TOK))
        row_total = jnp.sum(jnp.exp(prompt_scores - row_max[:, None]), 1) + jnp.sum(jnp.exp(own_scores - row_max.reshape(COMPS, MAXLEN, 1)), 2).reshape(TOK)
        log_total = row_max + jnp.log(row_total)
        prompt_prob = jnp.exp(prompt_scores - log_total[:, None])
        own_prob = jnp.exp(own_scores - log_total.reshape(COMPS, MAXLEN, 1))
        prompt_half = prompt_prob.astype(jnp.bfloat16)
        own_half = own_prob.astype(jnp.bfloat16)
        attended = jnp.dot(prompt_half, value_prompt, preferred_element_type=jnp.float32) + jnp.einsum("clm,cmd->cld", own_half.astype(jnp.float32), value_blocks).reshape(TOK, HD)
        row_delta = jnp.sum(grad_head.astype(jnp.float32) * attended, 1)
        prompt_dprob = jnp.dot(grad_head, value_prompt.T, preferred_element_type=jnp.float32)
        own_dprob = jnp.einsum("cld,cmd->clm", grad_blocks, value_blocks)
        prompt_dscore = (prompt_prob * (prompt_dprob - row_delta[:, None])).astype(jnp.bfloat16)
        own_dscore = (own_prob * (own_dprob - row_delta.reshape(COMPS, MAXLEN, 1))).astype(jnp.bfloat16)
        query_grads.append(softmax_scale * (jnp.dot(prompt_dscore, key_prompt, preferred_element_type=jnp.float32) + jnp.einsum("clm,cmd->cld", own_dscore.astype(jnp.float32), key_blocks).reshape(TOK, HD)))
        prompt_kgrad = prompt_kgrad + softmax_scale * jnp.dot(prompt_dscore.T, query_head, preferred_element_type=jnp.float32)
        prompt_vgrad = prompt_vgrad + jnp.dot(prompt_half.T, grad_head, preferred_element_type=jnp.float32)
        own_kgrad = own_kgrad + softmax_scale * jnp.einsum("clm,cld->cmd", own_dscore.astype(jnp.float32), query_blocks)
        own_vgrad = own_vgrad + jnp.einsum("clm,cld->cmd", own_half.astype(jnp.float32), grad_blocks)
    return jnp.stack(query_grads), prompt_kgrad, prompt_vgrad, own_kgrad.reshape(TOK, HD), own_vgrad.reshape(TOK, HD)


def split_heads(array):
    return array.reshape(array.shape[0], KVH, HD).transpose(1, 0, 2)


def join_heads(array):
    return array.transpose(1, 0, 2).reshape(array.shape[1], KVH * HD)


def reference(queries, comp_keys, comp_values, out_grad, prompt_keys, prompt_values, lengths):
    live_rows = (jnp.arange(MAXLEN, dtype=jnp.int32)[None, :] < BLK * lengths[:, None]).reshape(TOK)
    masked = out_grad * live_rows[:, None].astype(jnp.bfloat16)
    query_groups = queries.reshape(TOK, KVH, GROUP, HD).transpose(1, 2, 0, 3)
    grad_groups = masked.reshape(TOK, KVH, GROUP, HD).transpose(1, 2, 0, 3)
    query_grads, prompt_kgrad, prompt_vgrad, own_kgrad, own_vgrad = lax.map(group_pass, (query_groups, grad_groups, split_heads(prompt_keys), split_heads(prompt_values), split_heads(comp_keys), split_heads(comp_values)))
    grad_queries = query_grads.transpose(2, 0, 1, 3).reshape(TOK, QH * HD)
    return grad_queries, join_heads(prompt_kgrad), join_heads(prompt_vgrad), join_heads(own_kgrad), join_heads(own_vgrad)
```

```python
import jax
import jax.numpy as jnp
from jax import lax
from jax.experimental import pallas as pl
from jax.experimental.pallas import tpu as pltpu
from jax.sharding import PartitionSpec as P

HD = 128
BLK = 128
MAXLEN = 512
GROUP = 5
QB = 256
SCALE = HD ** (-0.5)
LOG2E = 1.4426950408889634
C2 = SCALE * LOG2E
F32 = jnp.float32
BF16 = jnp.bfloat16
VMEM_LIMIT = 40 * 1024 * 1024

NT = (((1,), (1,)), ((), ()))


def dot(a, b):
    return jnp.dot(a, b, preferred_element_type=F32)


def dot_nt(a, b):
    return lax.dot_general(a, b, NT, preferred_element_type=F32)


def causal_keep(rows, first_row):
    u = lax.broadcasted_iota(jnp.int32, (rows, QB), 0)
    i = lax.broadcasted_iota(jnp.int32, (rows, QB), 1)
    return u <= i


def lanes(head):
    return pl.ds(pl.multiple_of(head * HD, HD), HD)


def own_stats_kernel(
    len_ref, q_ref, g_ref, k_ref, v_ref, copy_ref, masked_ref, max_ref, sum_ref, del_ref
):
    live = lax.broadcasted_iota(jnp.int32, (MAXLEN, 1), 0) < BLK * len_ref[0]
    g = jnp.where(live, g_ref[...], jnp.zeros((), BF16))
    masked_ref[...] = g
    copy_ref[...] = q_ref[...]
    keep = causal_keep(QB, 0)
    for block in range(MAXLEN // QB):
        lo = block * QB
        hi = lo + QB
        q = q_ref[lo:hi, :]
        gb = g[lo:hi, :]
        diag = jnp.where(keep, dot_nt(k_ref[lo:hi, :], q), -jnp.inf)
        top = jnp.max(diag, axis=0, keepdims=True)
        if block:
            past = dot_nt(k_ref[0:lo, :], q)
            top = jnp.maximum(top, jnp.max(past, axis=0, keepdims=True))
        top = top * C2
        e = jnp.exp2(diag * C2 - top)
        total = jnp.sum(e, axis=0, keepdims=True)
        delta = jnp.sum(e * dot_nt(v_ref[lo:hi, :], gb), axis=0, keepdims=True)
        if block:
            e = jnp.exp2(past * C2 - top)
            total = total + jnp.sum(e, axis=0, keepdims=True)
            delta = delta + jnp.sum(e * dot_nt(v_ref[0:lo, :], gb), axis=0, keepdims=True)
        max_ref[0, :, lo:hi] = top
        sum_ref[0, :, lo:hi] = total
        del_ref[0, :, lo:hi] = delta


def prompt_kernel(
    core_ref, q_ref, g_ref, kv_ref, max_ref, sum_ref, del_ref,
    ds_ref, keep_ref, send_ref, lse_ref, delta_ref,
    grad_ref, *scratch,
):
    tokens = kv_ref.shape[0]
    tile = 64
    sets = (scratch[0:5], scratch[5:10])

    def rows(block):
        return slice(block * QB, (block + 1) * QB)

    def scores(head, block):
        s_ref, dp_ref, _, _, top_ref = sets[block]
        s = dot_nt(kv_ref[:, 0:HD], q_ref[rows(block), lanes(head)])
        s_ref[...] = s
        top_ref[...] = jnp.max(s.reshape(tokens // 8, 8, QB), axis=0)
        dp_ref[...] = dot_nt(kv_ref[:, HD:], g_ref[rows(block), lanes(head)])

    def softmax(head, block):
        s_ref, dp_ref, p_ref, d_ref, top_ref = sets[block]
        own_top = max_ref[head, :, rows(block)]
        top = jnp.max(top_ref[...], axis=0, keepdims=True) * C2
        top = jnp.maximum(top, own_top)
        own = jnp.exp2(own_top - top)
        total = jnp.zeros((8, QB), F32)
        delta = jnp.zeros((8, QB), F32)
        for t in range(0, tokens, tile):
            e = jnp.exp2(s_ref[t : t + tile, :] * C2 - top)
            s_ref[t : t + tile, :] = e
            total = total + jnp.sum(e.reshape(tile // 8, 8, QB), axis=0)
            ed = e * dp_ref[t : t + tile, :]
            delta = delta + jnp.sum(ed.reshape(tile // 8, 8, QB), axis=0)
        total = jnp.sum(total, axis=0, keepdims=True) + own * sum_ref[head, :, rows(block)]
        inverse = 1.0 / total
        delta = jnp.sum(delta, axis=0, keepdims=True) + own * del_ref[head, :, rows(block)]
        delta = delta * inverse
        lse_ref[head, :, rows(block)] = top + jnp.log2(total)
        delta_ref[head, :, rows(block)] = delta
        for t in range(0, tokens, tile):
            p = s_ref[t : t + tile, :] * inverse
            p_ref[t : t + tile, :] = p.astype(BF16)
            ds = (p * (dp_ref[t : t + tile, :] - delta)).astype(BF16)
            d_ref[t : t + tile, :] = ds
            ds_ref[head, t : t + tile, rows(block)] = ds

    def grads(head, block):
        _, _, p_ref, d_ref, _ = sets[block]
        grad_ref[:, 0:HD] += dot(d_ref[...], q_ref[rows(block), lanes(head)])
        grad_ref[:, HD:] += dot(p_ref[...], g_ref[rows(block), lanes(head)])

    grad_ref[...] = jnp.zeros_like(grad_ref)
    scores(0, 0)
    scores(0, 1)
    softmax(0, 0)

    def body(head, carry):
        scores(head, 0)
        softmax(head - 1, 1)
        grads(head - 1, 0)
        scores(head, 1)
        softmax(head, 0)
        grads(head - 1, 1)
        return carry

    lax.fori_loop(1, GROUP, body, 0)
    softmax(GROUP - 1, 1)
    grads(GROUP - 1, 0)
    grads(GROUP - 1, 1)

    half = tokens // 2
    core = core_ref[0]
    for out, side in ((keep_ref, core), (send_ref, 1 - core)):
        part = grad_ref[pl.ds(pl.multiple_of(side * half, half), half), :]
        out[:, 0:HD] = part[:, 0:HD] * SCALE
        out[:, HD:] = part[:, HD:]


def tail_kernel(
    q_ref, g_ref, k_ref, v_ref, lse_ref, delta_ref, ds_ref, kv_ref, dq_ref, dk_ref, dv_ref
):
    head = pl.program_id(0)

    @pl.when(head == 0)
    def _():
        dk_ref[...] = jnp.zeros_like(dk_ref)
        dv_ref[...] = jnp.zeros_like(dv_ref)

    keep = causal_keep(QB, 0)
    keys_t = k_ref[...].T
    grad = dot(kv_ref[:, 0:HD].T, ds_ref[head])
    for block in range(MAXLEN // QB):
        lo = block * QB
        hi = lo + QB
        q = q_ref[lo:hi, lanes(head)]
        gb = g_ref[lo:hi, lanes(head)]
        lse = lse_ref[head, :, lo:hi]
        delta = delta_ref[head, :, lo:hi]
        p = jnp.exp2(dot_nt(k_ref[0:hi, :], q) * C2 - lse)
        last = jnp.where(keep, p[lo:hi], 0.0)
        p = jnp.concatenate([p[0:lo], last], axis=0) if block else last
        ds = (p * (dot_nt(v_ref[0:hi, :], gb) - delta)).astype(BF16)
        dv_ref[0:hi, :] += dot(p.astype(BF16), gb)
        dk_ref[0:hi, :] += dot(ds, q)
        part = grad[:, lo:hi] + dot(keys_t[:, 0:hi], ds)
        dq_ref[lo:hi, :] = part.T * SCALE

    @pl.when(head == GROUP - 1)
    def _():
        dk_ref[...] = dk_ref[...] * SCALE


def whole(shape):
    return pl.BlockSpec(shape, lambda h: (0,) * len(shape))


HEAD = pl.BlockSpec((MAXLEN, HD), lambda h: (0, h))
ROW = pl.BlockSpec((1, 1, MAXLEN), lambda h: (h, 0, 0))


def params():
    return pltpu.CompilerParams(
        dimension_semantics=("arbitrary",), vmem_limit_bytes=VMEM_LIMIT
    )


def cost(flops, exps, moved):
    return pl.CostEstimate(flops=flops, transcendentals=exps, bytes_accessed=moved)


def struct(shape, dtype):
    return jax.ShapeDtypeStruct(shape, dtype)


def vmem_struct(shape, dtype):
    return pltpu.VMEM(shape, dtype)


def vmem(x):
    return pltpu.with_memory_space_constraint(x, pltpu.VMEM)


def hbm(x):
    return pltpu.with_memory_space_constraint(x, pltpu.HBM)


SMEM = pl.BlockSpec(memory_space=pltpu.SMEM)
VMEM = pl.BlockSpec(memory_space=pltpu.VMEM)


def per_device(queries, comp_keys, comp_values, out_grad, prompt_keys, prompt_values, lengths):
    shard = prompt_keys.shape[0]
    devices = lax.axis_size("comp")
    chips = devices // 2
    ring = devices // 4
    tokens = devices * shard
    half = tokens // 2
    width = GROUP * HD

    own = jnp.concatenate([prompt_keys, prompt_values], axis=1)
    along_y = [[y * 4 + rest for y in range(ring)] for rest in range(4)]
    rest_of = [[y * 4 + z * 2 + core for core in range(2) for z in range(2)] for y in range(ring)]
    gathered = lax.all_gather(own, "comp", axis=0, tiled=True, axis_index_groups=along_y)
    prompt = lax.all_gather(gathered, "comp", axis=0, tiled=True, axis_index_groups=rest_of)
    core = (lax.axis_index("comp") % 2).reshape(1).astype(jnp.int32)

    stat = struct((GROUP, 1, MAXLEN), F32)
    copied, masked, own_max, own_sum, own_del = pl.pallas_call(
        own_stats_kernel,
        grid=(GROUP,),
        in_specs=[SMEM, HEAD, HEAD, whole((MAXLEN, HD)), whole((MAXLEN, HD))],
        out_specs=[HEAD, HEAD, ROW, ROW, ROW],
        out_shape=[
            vmem_struct((MAXLEN, width), BF16), vmem_struct((MAXLEN, width), BF16),
            stat, stat, stat,
        ],
        compiler_params=params(),
        cost_estimate=cost(GROUP * 4 * 384 * 512 * HD, GROUP * 384 * 512, 2**21),
        name="own_stats",
    )(lengths, hbm(queries), hbm(out_grad), hbm(comp_keys), hbm(comp_values))

    dscore, grad_keep, grad_send, lse, delta = pl.pallas_call(
        prompt_kernel,
        in_specs=[SMEM] + [VMEM] * 6,
        out_specs=[VMEM] * 5,
        out_shape=[
            vmem_struct((GROUP, tokens, MAXLEN), BF16),
            struct((half, 2 * HD), F32), struct((half, 2 * HD), F32), stat, stat,
        ],
        scratch_shapes=[pltpu.VMEM((tokens, 2 * HD), F32)]
        + [
            pltpu.VMEM((tokens, QB), F32),
            pltpu.VMEM((tokens, QB), F32),
            pltpu.VMEM((tokens, QB), BF16),
            pltpu.VMEM((tokens, QB), BF16),
            pltpu.VMEM((8, QB), F32),
        ]
        * 2,
        compiler_params=pltpu.CompilerParams(vmem_limit_bytes=VMEM_LIMIT),
        cost_estimate=cost(GROUP * 8 * 1024 * 512 * HD, GROUP * 1024 * 512, 2**23),
        name="prompt",
    )(core, vmem(copied), vmem(masked), prompt, own_max, own_sum, own_del)

    swap = [(d, d ^ 1) for d in range(devices)]
    received = lax.ppermute(grad_send, "comp", swap)
    chip_sum = (grad_keep + received).astype(BF16).reshape(chips, shard, 2 * HD)
    same_core = [
        [y * 4 + z * 2 + side for z in range(2) for y in range(ring)] for side in range(2)
    ]
    arrived = lax.all_to_all(chip_sum, "comp", 0, 0, axis_index_groups=same_core, tiled=True)
    grad_prompt = jnp.sum(arrived.astype(F32), axis=0)

    grad_queries, grad_comp_keys, grad_comp_values = pl.pallas_call(
        tail_kernel,
        grid=(GROUP,),
        in_specs=[VMEM, VMEM, whole((MAXLEN, HD)), whole((MAXLEN, HD)), VMEM, VMEM, VMEM, VMEM],
        out_specs=[HEAD, whole((MAXLEN, HD)), whole((MAXLEN, HD))],
        out_shape=[
            struct((MAXLEN, width), F32),
            struct((MAXLEN, HD), F32), struct((MAXLEN, HD), F32),
        ],
        compiler_params=params(),
        cost_estimate=cost(GROUP * 4 * 1024 * 512 * HD, GROUP * 384 * 512, 2**23),
        name="tail",
    )(
        vmem(copied), vmem(masked), hbm(comp_keys), hbm(comp_values), lse, delta,
        vmem(dscore), prompt,
    )

    return (
        grad_queries,
        grad_prompt[:, 0:HD],
        grad_prompt[:, HD:],
        grad_comp_keys,
        grad_comp_values,
    )


def solution(mesh):
    rows = P(("grp", "comp"), "tp")
    return jax.shard_map(
        per_device,
        mesh=mesh,
        in_specs=(rows,) * 6 + (P(("grp", "comp")),),
        out_specs=(rows,) * 5,
        check_vma=False,
    )
```

```python
import jax
import jax.numpy as jnp
from jax import lax
from jax.experimental import pallas as pl
from jax.experimental.pallas import tpu as pltpu
from jax.sharding import PartitionSpec as P

HD = 128
BLK = 128
MAXLEN = 512
GROUP = 5
QB = 256
SHARD = 32
SCALE = HD ** (-0.5)
LOG2E = 1.4426950408889634
C2 = SCALE * LOG2E
F32 = jnp.float32
BF16 = jnp.bfloat16
VMEM_LIMIT = 40 * 1024 * 1024

NT = (((1,), (1,)), ((), ()))


def dot(a, b):
    return jnp.dot(a, b, preferred_element_type=F32)


def dot_nt(a, b):
    return lax.dot_general(a, b, NT, preferred_element_type=F32)


def causal_keep(rows, first_row):
    u = lax.broadcasted_iota(jnp.int32, (rows, QB), 0)
    i = lax.broadcasted_iota(jnp.int32, (rows, QB), 1)
    return u <= i


def lanes(head):
    return pl.ds(pl.multiple_of(head * HD, HD), HD)


def spread_kernel(k_ref, v_ref, out_ref):
    for chip in range(out_ref.shape[0]):
        out_ref[chip, :, 0:HD] = k_ref[...]
        out_ref[chip, :, HD:] = v_ref[...]


def own_stats_kernel(
    len_ref, q_ref, g_ref, k_ref, v_ref, copy_ref, masked_ref, max_ref, sum_ref, del_ref
):
    live = lax.broadcasted_iota(jnp.int32, (MAXLEN, 1), 0) < BLK * len_ref[0]
    g = jnp.where(live, g_ref[...], jnp.zeros((), BF16))
    masked_ref[...] = g
    copy_ref[...] = q_ref[...]
    keep = causal_keep(QB, 0)
    for block in range(MAXLEN // QB):
        lo = block * QB
        hi = lo + QB
        q = q_ref[lo:hi, :]
        gb = g[lo:hi, :]
        diag = jnp.where(keep, dot_nt(k_ref[lo:hi, :], q), -jnp.inf)
        top = jnp.max(diag, axis=0, keepdims=True)
        if block:
            past = dot_nt(k_ref[0:lo, :], q)
            top = jnp.maximum(top, jnp.max(past, axis=0, keepdims=True))
        top = top * C2
        e = jnp.exp2(diag * C2 - top)
        total = jnp.sum(e, axis=0, keepdims=True)
        delta = jnp.sum(e * dot_nt(v_ref[lo:hi, :], gb), axis=0, keepdims=True)
        if block:
            e = jnp.exp2(past * C2 - top)
            total = total + jnp.sum(e, axis=0, keepdims=True)
            delta = delta + jnp.sum(e * dot_nt(v_ref[0:lo, :], gb), axis=0, keepdims=True)
        max_ref[0, :, lo:hi] = top
        sum_ref[0, :, lo:hi] = total
        del_ref[0, :, lo:hi] = delta


def prompt_kernel(
    q_ref, g_ref, mine_ref, other_ref, max_ref, sum_ref, del_ref,
    dq_ref, keep_ref, send_ref, lse_ref, delta_ref,
    grad_ref, kt_ref, kv_ref, *scratch,
):
    half = mine_ref.shape[0]
    tokens = 2 * half
    tile = 64
    sets = (scratch[0:5], scratch[5:10])

    def rows(block):
        return slice(block * QB, (block + 1) * QB)

    def scores(head, block):
        s_ref, dp_ref, _, _, top_ref = sets[block]
        s = dot_nt(kv_ref[:, 0:HD], q_ref[rows(block), lanes(head)])
        s_ref[...] = s
        top_ref[...] = jnp.max(s.reshape(tokens // 8, 8, QB), axis=0)
        dp_ref[...] = dot_nt(kv_ref[:, HD:], g_ref[rows(block), lanes(head)])

    def softmax(head, block):
        s_ref, dp_ref, p_ref, d_ref, top_ref = sets[block]
        own_top = max_ref[head, :, rows(block)]
        top = jnp.max(top_ref[...], axis=0, keepdims=True) * C2
        top = jnp.maximum(top, own_top)
        own = jnp.exp2(own_top - top)
        total = jnp.zeros((8, QB), F32)
        delta = jnp.zeros((8, QB), F32)
        for t in range(0, tokens, tile):
            e = jnp.exp2(s_ref[t : t + tile, :] * C2 - top)
            total = total + jnp.sum(e.reshape(tile // 8, 8, QB), axis=0)
            ed = e * dp_ref[t : t + tile, :]
            delta = delta + jnp.sum(ed.reshape(tile // 8, 8, QB), axis=0)
        total = jnp.sum(total, axis=0, keepdims=True) + own * sum_ref[head, :, rows(block)]
        delta = jnp.sum(delta, axis=0, keepdims=True) + own * del_ref[head, :, rows(block)]
        delta = delta * (1.0 / total)
        lse = top + jnp.log2(total)
        lse_ref[head, :, rows(block)] = lse
        delta_ref[head, :, rows(block)] = delta
        for t in range(0, tokens, tile):
            p = jnp.exp2(s_ref[t : t + tile, :] * C2 - lse)
            p_ref[t : t + tile, :] = p.astype(BF16)
            d_ref[t : t + tile, :] = (p * (dp_ref[t : t + tile, :] - delta)).astype(BF16)

    def grads(head, block):
        _, _, p_ref, d_ref, _ = sets[block]
        grad_ref[0:HD, :] += dot_nt(q_ref[rows(block), lanes(head)].T, d_ref[...])
        grad_ref[HD:, :] += dot_nt(g_ref[rows(block), lanes(head)].T, p_ref[...])
        dq_ref[head, :, rows(block)] = dot(kt_ref[...], d_ref[...])

    kv_ref[0:half, :] = mine_ref[...]
    kv_ref[half:, :] = other_ref[...]
    kt_ref[...] = kv_ref[:, 0:HD].T
    grad_ref[...] = jnp.zeros_like(grad_ref)
    scores(0, 0)
    scores(0, 1)
    softmax(0, 0)

    def body(head, carry):
        scores(head, 0)
        softmax(head - 1, 1)
        grads(head - 1, 0)
        scores(head, 1)
        softmax(head, 0)
        grads(head - 1, 1)
        return carry

    lax.fori_loop(1, GROUP, body, 0)
    softmax(GROUP - 1, 1)
    grads(GROUP - 1, 0)
    grads(GROUP - 1, 1)

    for base, out in ((0, keep_ref), (half, send_ref)):
        for t in range(0, half, HD):
            take = slice(base + t, base + t + HD)
            out[t : t + HD, 0:HD] = grad_ref[0:HD, take].T * SCALE
            out[t : t + HD, HD:] = grad_ref[HD:, take].T


def own_grad_kernel(
    q_ref, g_ref, k_ref, v_ref, lse_ref, delta_ref, past_ref, dq_ref, dk_ref, dv_ref
):
    head = pl.program_id(0)

    @pl.when(head == 0)
    def _():
        dk_ref[...] = jnp.zeros_like(dk_ref)
        dv_ref[...] = jnp.zeros_like(dv_ref)

    keep = causal_keep(QB, 0)
    keys_t = k_ref[...].T
    for block in range(MAXLEN // QB):
        lo = block * QB
        hi = lo + QB
        q = q_ref[lo:hi, lanes(head)]
        gb = g_ref[lo:hi, lanes(head)]
        lse = lse_ref[head, :, lo:hi]
        delta = delta_ref[head, :, lo:hi]
        p = jnp.exp2(dot_nt(k_ref[0:hi, :], q) * C2 - lse)
        last = jnp.where(keep, p[lo:hi], 0.0)
        p = jnp.concatenate([p[0:lo], last], axis=0) if block else last
        ds = (p * (dot_nt(v_ref[0:hi, :], gb) - delta)).astype(BF16)
        dv_ref[0:hi, :] += dot(p.astype(BF16), gb)
        dk_ref[0:hi, :] += dot(ds, q)
        part = past_ref[head, :, lo:hi] + dot(keys_t[:, 0:hi], ds)
        dq_ref[lo:hi, :] = part.T * SCALE

    @pl.when(head == GROUP - 1)
    def _():
        dk_ref[...] = dk_ref[...] * SCALE


def whole(shape):
    return pl.BlockSpec(shape, lambda h: (0,) * len(shape))


HEAD = pl.BlockSpec((MAXLEN, HD), lambda h: (0, h))
ROW = pl.BlockSpec((1, 1, MAXLEN), lambda h: (h, 0, 0))


def params():
    return pltpu.CompilerParams(
        dimension_semantics=("arbitrary",), vmem_limit_bytes=VMEM_LIMIT
    )


def cost(flops, exps, moved):
    return pl.CostEstimate(flops=flops, transcendentals=exps, bytes_accessed=moved)


def struct(shape, dtype):
    return jax.ShapeDtypeStruct(shape, dtype)


def vmem_struct(shape, dtype):
    return pltpu.VMEM(shape, dtype)


def vmem(x):
    return pltpu.with_memory_space_constraint(x, pltpu.VMEM)


def hbm(x):
    return pltpu.with_memory_space_constraint(x, pltpu.HBM)


SMEM = pl.BlockSpec(memory_space=pltpu.SMEM)
VMEM = pl.BlockSpec(memory_space=pltpu.VMEM)


def per_device(queries, comp_keys, comp_values, out_grad, prompt_keys, prompt_values, lengths):
    devices = lax.axis_size("comp")
    half = devices * SHARD // 2
    tokens = 2 * half
    width = GROUP * HD

    chips = devices // 2
    swap = [(d, d ^ 1) for d in range(devices)]
    same_core = [[2 * chip + core for chip in range(chips)] for core in range(2)]
    spread = pl.pallas_call(
        spread_kernel,
        in_specs=[VMEM, VMEM],
        out_specs=VMEM,
        out_shape=struct((chips, SHARD, 2 * HD), BF16),
        name="spread",
    )(hbm(prompt_keys), hbm(prompt_values))
    mine = lax.all_to_all(spread, "comp", 0, 0, axis_index_groups=same_core, tiled=True)
    mine = mine.reshape(half, 2 * HD)

    stat = struct((GROUP, 1, MAXLEN), F32)
    copied, masked, own_max, own_sum, own_del = pl.pallas_call(
        own_stats_kernel,
        grid=(GROUP,),
        in_specs=[SMEM, HEAD, HEAD, whole((MAXLEN, HD)), whole((MAXLEN, HD))],
        out_specs=[HEAD, HEAD, ROW, ROW, ROW],
        out_shape=[
            vmem_struct((MAXLEN, width), BF16), vmem_struct((MAXLEN, width), BF16),
            stat, stat, stat,
        ],
        compiler_params=params(),
        cost_estimate=cost(GROUP * 4 * 384 * 512 * HD, GROUP * 384 * 512, 2**21),
        name="own_stats",
    )(lengths, hbm(queries), hbm(out_grad), hbm(comp_keys), hbm(comp_values))

    mine, masked = lax.optimization_barrier((mine, masked))
    other = lax.ppermute(mine, "comp", swap)

    past, grad_keep, grad_send, lse, delta = pl.pallas_call(
        prompt_kernel,
        in_specs=[VMEM] * 7,
        out_specs=[VMEM] * 5,
        out_shape=[
            struct((GROUP, HD, MAXLEN), F32),
            struct((half, 2 * HD), F32), struct((half, 2 * HD), F32), stat, stat,
        ],
        scratch_shapes=[
            pltpu.VMEM((2 * HD, tokens), F32),
            pltpu.VMEM((HD, tokens), BF16),
            pltpu.VMEM((tokens, 2 * HD), BF16),
        ]
        + [
            pltpu.VMEM((tokens, QB), F32),
            pltpu.VMEM((tokens, QB), F32),
            pltpu.VMEM((tokens, QB), BF16),
            pltpu.VMEM((tokens, QB), BF16),
            pltpu.VMEM((8, QB), F32),
        ]
        * 2,
        compiler_params=pltpu.CompilerParams(vmem_limit_bytes=VMEM_LIMIT),
        cost_estimate=cost(GROUP * 10 * 1024 * 512 * HD, GROUP * 2048 * 512, 2**22),
        name="prompt",
    )(vmem(copied), vmem(masked), mine, other, own_max, own_sum, own_del)

    received = lax.ppermute(grad_send, "comp", swap)
    total = (grad_keep + received).astype(BF16).reshape(chips, SHARD, 2 * HD)
    arrived = lax.all_to_all(total, "comp", 0, 0, axis_index_groups=same_core, tiled=True)
    grad_prompt = jnp.sum(arrived.astype(F32), axis=0)

    grad_queries, grad_comp_keys, grad_comp_values = pl.pallas_call(
        own_grad_kernel,
        grid=(GROUP,),
        in_specs=[VMEM, VMEM, whole((MAXLEN, HD)), whole((MAXLEN, HD)), VMEM, VMEM, VMEM],
        out_specs=[HEAD, whole((MAXLEN, HD)), whole((MAXLEN, HD))],
        out_shape=[
            struct((MAXLEN, width), F32),
            struct((MAXLEN, HD), F32), struct((MAXLEN, HD), F32),
        ],
        compiler_params=params(),
        cost_estimate=cost(GROUP * 10 * 384 * 512 * HD, GROUP * 384 * 512, 2**22),
        name="own_grad",
    )(
        vmem(copied), vmem(masked), hbm(comp_keys), hbm(comp_values), lse, delta, past,
    )

    return (
        grad_queries,
        grad_prompt[:, 0:HD],
        grad_prompt[:, HD:],
        grad_comp_keys,
        grad_comp_values,
    )


def solution(mesh):
    rows = P(("grp", "comp"), "tp")
    return jax.shard_map(
        per_device,
        mesh=mesh,
        in_specs=(rows,) * 6 + (P(("grp", "comp")),),
        out_specs=(rows,) * 5,
        check_vma=False,
    )
```

```python
import jax
import jax.numpy as jnp
from jax import lax
from jax.experimental import pallas as pl
from jax.experimental.pallas import tpu as pltpu
from jax.sharding import PartitionSpec as P

HD = 128
BLK = 128
MAXLEN = 512
GROUP = 5
QB = 256
SHARD = 32
SCALE = HD ** (-0.5)
LOG2E = 1.4426950408889634
C2 = SCALE * LOG2E
F32 = jnp.float32
BF16 = jnp.bfloat16
VMEM_LIMIT = 40 * 1024 * 1024

NT = (((1,), (1,)), ((), ()))


def dot(a, b):
    return jnp.dot(a, b, preferred_element_type=F32)


def dot_nt(a, b):
    return lax.dot_general(a, b, NT, preferred_element_type=F32)


def causal_keep(rows, first_row):
    u = lax.broadcasted_iota(jnp.int32, (rows, QB), 0)
    i = lax.broadcasted_iota(jnp.int32, (rows, QB), 1)
    return u <= i


def lanes(head):
    return pl.ds(pl.multiple_of(head * HD, HD), HD)


def spread_kernel(k_ref, v_ref, out_ref, held_ref, sems):
    copies = [
        pltpu.make_async_copy(src, held_ref.at[i], sems.at[i])
        for i, src in enumerate((k_ref, v_ref))
    ]
    for copy in copies:
        copy.start()
    for copy in copies:
        copy.wait()
    for chip in range(out_ref.shape[0]):
        out_ref[chip, :, 0:HD] = held_ref[0]
        out_ref[chip, :, HD:] = held_ref[1]


def own_stats_kernel(
    len_ref, q_ref, g_ref, k_ref, v_ref, copy_ref, masked_ref, max_ref, sum_ref, del_ref
):
    live = lax.broadcasted_iota(jnp.int32, (MAXLEN, 1), 0) < BLK * len_ref[0]
    g = jnp.where(live, g_ref[...], jnp.zeros((), BF16))
    masked_ref[...] = g
    copy_ref[...] = q_ref[...]
    keep = causal_keep(QB, 0)
    for block in range(MAXLEN // QB):
        lo = block * QB
        hi = lo + QB
        q = q_ref[lo:hi, :]
        gb = g[lo:hi, :]
        diag = jnp.where(keep, dot_nt(k_ref[lo:hi, :], q), -jnp.inf)
        top = jnp.max(diag, axis=0, keepdims=True)
        if block:
            past = dot_nt(k_ref[0:lo, :], q)
            top = jnp.maximum(top, jnp.max(past, axis=0, keepdims=True))
        top = top * C2
        e = jnp.exp2(diag * C2 - top)
        total = jnp.sum(e, axis=0, keepdims=True)
        delta = jnp.sum(e * dot_nt(v_ref[lo:hi, :], gb), axis=0, keepdims=True)
        if block:
            e = jnp.exp2(past * C2 - top)
            total = total + jnp.sum(e, axis=0, keepdims=True)
            delta = delta + jnp.sum(e * dot_nt(v_ref[0:lo, :], gb), axis=0, keepdims=True)
        max_ref[0, :, lo:hi] = top
        sum_ref[0, :, lo:hi] = total
        del_ref[0, :, lo:hi] = delta


def prompt_kernel(
    q_ref, g_ref, mine_ref, other_ref, max_ref, sum_ref, del_ref,
    dq_ref, keep_ref, send_ref, lse_ref, delta_ref,
    grad_ref, kt_ref, vt_ref, ks_ref, v_ref, *scratch,
):
    half = mine_ref.shape[0]
    tokens = 2 * half
    tile = 64
    sets = (scratch[0:5], scratch[5:10])

    def rows(block):
        return slice(block * QB, (block + 1) * QB)

    def scores(head, block):
        s_ref, _, _, _, top_ref = sets[block]
        q = q_ref[rows(block), lanes(head)]
        s = dot_nt(ks_ref[...], jnp.concatenate([q, q], axis=1))
        s_ref[...] = s
        top_ref[...] = jnp.max(s.reshape(tokens // 8, 8, QB), axis=0)

    def softmax(head, block):
        s_ref, prob_ref, p_ref, _, top_ref = sets[block]
        own_top = max_ref[head, :, rows(block)]
        top = jnp.maximum(jnp.max(top_ref[...], axis=0, keepdims=True), own_top)
        own = jnp.exp2(own_top - top)
        total = jnp.zeros((8, QB), F32)
        for t in range(0, tokens, tile):
            e = jnp.exp2(s_ref[t : t + tile, :] - top)
            s_ref[t : t + tile, :] = e
            total = total + jnp.sum(e.reshape(tile // 8, 8, QB), axis=0)
        total = jnp.sum(total, axis=0, keepdims=True) + own * sum_ref[head, :, rows(block)]
        inverse = 1.0 / total
        lse_ref[head, :, rows(block)] = top + jnp.log2(total)
        for t in range(0, tokens, tile):
            p = s_ref[t : t + tile, :] * inverse
            prob_ref[t : t + tile, :] = p
            p_ref[t : t + tile, :] = p.astype(BF16)
        attended = dot(vt_ref[...], p_ref[...])
        g = g_ref[rows(block), lanes(head)].T.astype(F32)
        delta = jnp.sum(attended * g, axis=0, keepdims=True)
        delta_ref[head, :, rows(block)] = delta + own * inverse * del_ref[head, :, rows(block)]

    def grads(head, block):
        _, prob_ref, p_ref, d_ref, _ = sets[block]
        q = q_ref[rows(block), lanes(head)]
        g = g_ref[rows(block), lanes(head)]
        delta = delta_ref[head, :, rows(block)]
        ds = prob_ref[...] * (dot_nt(v_ref[...], g) - delta)
        d_ref[...] = ds.astype(BF16)
        grad_ref[HD:, :] += dot_nt(g.T, p_ref[...])
        grad_ref[0:HD, :] += dot_nt(q.T, d_ref[...])
        dq_ref[head, :, rows(block)] = dot(kt_ref[...], d_ref[...])

    for first, side_ref in ((0, mine_ref), (half, other_ref)):
        part = slice(first, first + half)
        keys = side_ref[:, 0:HD]
        values = side_ref[:, HD:]
        kt_ref[:, part] = keys.T
        vt_ref[:, part] = values.T
        v_ref[part, :] = values
        scaled = keys.astype(F32) * C2
        high = scaled.astype(BF16)
        ks_ref[part, 0:HD] = high
        ks_ref[part, HD:] = (scaled - high.astype(F32)).astype(BF16)
    grad_ref[...] = jnp.zeros_like(grad_ref)

    scores(0, 0)
    scores(0, 1)
    softmax(0, 0)

    def body(head, carry):
        scores(head, 0)
        softmax(head - 1, 1)
        grads(head - 1, 0)
        scores(head, 1)
        softmax(head, 0)
        grads(head - 1, 1)
        return carry

    lax.fori_loop(1, GROUP, body, 0)
    softmax(GROUP - 1, 1)
    grads(GROUP - 1, 0)
    grads(GROUP - 1, 1)

    for base, out in ((0, keep_ref), (half, send_ref)):
        for t in range(0, half, HD):
            take = slice(base + t, base + t + HD)
            out[t : t + HD, 0:HD] = grad_ref[0:HD, take].T * SCALE
            out[t : t + HD, HD:] = grad_ref[HD:, take].T


def own_grad_kernel(
    q_ref, g_ref, k_ref, v_ref, lse_ref, delta_ref, past_ref, dq_ref, dk_ref, dv_ref
):
    head = pl.program_id(0)

    @pl.when(head == 0)
    def _():
        dk_ref[...] = jnp.zeros_like(dk_ref)
        dv_ref[...] = jnp.zeros_like(dv_ref)

    keep = causal_keep(QB, 0)
    keys_t = k_ref[...].T
    for block in range(MAXLEN // QB):
        lo = block * QB
        hi = lo + QB
        q = q_ref[lo:hi, lanes(head)]
        gb = g_ref[lo:hi, lanes(head)]
        lse = lse_ref[head, :, lo:hi]
        delta = delta_ref[head, :, lo:hi]
        p = jnp.exp2(dot_nt(k_ref[0:hi, :], q) * C2 - lse)
        last = jnp.where(keep, p[lo:hi], 0.0)
        p = jnp.concatenate([p[0:lo], last], axis=0) if block else last
        ds = (p * (dot_nt(v_ref[0:hi, :], gb) - delta)).astype(BF16)
        dv_ref[0:hi, :] += dot(p.astype(BF16), gb)
        dk_ref[0:hi, :] += dot(ds, q)
        part = past_ref[head, :, lo:hi] + dot(keys_t[:, 0:hi], ds)
        dq_ref[lo:hi, :] = part.T * SCALE

    @pl.when(head == GROUP - 1)
    def _():
        dk_ref[...] = dk_ref[...] * SCALE


def whole(shape):
    return pl.BlockSpec(shape, lambda h: (0,) * len(shape))


HEAD = pl.BlockSpec((MAXLEN, HD), lambda h: (0, h))
ROW = pl.BlockSpec((1, 1, MAXLEN), lambda h: (h, 0, 0))


def params():
    return pltpu.CompilerParams(
        dimension_semantics=("arbitrary",), vmem_limit_bytes=VMEM_LIMIT
    )


def cost(flops, exps, moved):
    return pl.CostEstimate(flops=flops, transcendentals=exps, bytes_accessed=moved)


def struct(shape, dtype):
    return jax.ShapeDtypeStruct(shape, dtype)


def vmem_struct(shape, dtype):
    return pltpu.VMEM(shape, dtype)


def vmem(x):
    return pltpu.with_memory_space_constraint(x, pltpu.VMEM)


def hbm(x):
    return pltpu.with_memory_space_constraint(x, pltpu.HBM)


SMEM = pl.BlockSpec(memory_space=pltpu.SMEM)
VMEM = pl.BlockSpec(memory_space=pltpu.VMEM)


def per_device(queries, comp_keys, comp_values, out_grad, prompt_keys, prompt_values, lengths):
    devices = lax.axis_size("comp")
    half = devices * SHARD // 2
    tokens = 2 * half
    width = GROUP * HD

    chips = devices // 2
    swap = [(d, d ^ 1) for d in range(devices)]
    same_core = [[2 * chip + core for chip in range(chips)] for core in range(2)]
    spread = pl.pallas_call(
        spread_kernel,
        in_specs=[pl.BlockSpec(memory_space=pltpu.HBM)] * 2,
        out_specs=VMEM,
        out_shape=struct((chips, SHARD, 2 * HD), BF16),
        scratch_shapes=[pltpu.VMEM((2, SHARD, HD), BF16), pltpu.SemaphoreType.DMA((2,))],
        name="spread",
    )(prompt_keys, prompt_values)
    mine = lax.all_to_all(spread, "comp", 0, 0, axis_index_groups=same_core, tiled=True)
    mine = mine.reshape(half, 2 * HD)

    stat = struct((GROUP, 1, MAXLEN), F32)
    copied, masked, own_max, own_sum, own_del = pl.pallas_call(
        own_stats_kernel,
        grid=(GROUP,),
        in_specs=[SMEM, HEAD, HEAD, whole((MAXLEN, HD)), whole((MAXLEN, HD))],
        out_specs=[HEAD, HEAD, ROW, ROW, ROW],
        out_shape=[
            vmem_struct((MAXLEN, width), BF16), vmem_struct((MAXLEN, width), BF16),
            stat, stat, stat,
        ],
        compiler_params=params(),
        cost_estimate=cost(GROUP * 4 * 384 * 512 * HD, GROUP * 384 * 512, 2**21),
        name="own_stats",
    )(lengths, hbm(queries), hbm(out_grad), hbm(comp_keys), hbm(comp_values))

    mine, masked = lax.optimization_barrier((mine, masked))
    other = lax.ppermute(mine, "comp", swap)

    past, grad_keep, grad_send, lse, delta = pl.pallas_call(
        prompt_kernel,
        in_specs=[VMEM] * 7,
        out_specs=[VMEM] * 5,
        out_shape=[
            struct((GROUP, HD, MAXLEN), F32),
            struct((half, 2 * HD), F32), struct((half, 2 * HD), F32), stat, stat,
        ],
        scratch_shapes=[
            pltpu.VMEM((2 * HD, tokens), F32),
            pltpu.VMEM((HD, tokens), BF16),
            pltpu.VMEM((HD, tokens), BF16),
            pltpu.VMEM((tokens, 2 * HD), BF16),
            pltpu.VMEM((tokens, HD), BF16),
        ]
        + [
            pltpu.VMEM((tokens, QB), F32),
            pltpu.VMEM((tokens, QB), F32),
            pltpu.VMEM((tokens, QB), BF16),
            pltpu.VMEM((tokens, QB), BF16),
            pltpu.VMEM((8, QB), F32),
        ]
        * 2,
        compiler_params=pltpu.CompilerParams(vmem_limit_bytes=VMEM_LIMIT),
        cost_estimate=cost(GROUP * 10 * 1024 * 512 * HD, GROUP * 2048 * 512, 2**22),
        name="prompt",
    )(vmem(copied), vmem(masked), mine, other, own_max, own_sum, own_del)

    received = lax.ppermute(grad_send, "comp", swap)
    total = (grad_keep + received).astype(BF16).reshape(chips, SHARD, 2 * HD)
    arrived = lax.all_to_all(total, "comp", 0, 0, axis_index_groups=same_core, tiled=True)
    grad_prompt = jnp.sum(arrived.astype(F32), axis=0)

    grad_queries, grad_comp_keys, grad_comp_values = pl.pallas_call(
        own_grad_kernel,
        grid=(GROUP,),
        in_specs=[VMEM, VMEM, whole((MAXLEN, HD)), whole((MAXLEN, HD)), VMEM, VMEM, VMEM],
        out_specs=[HEAD, whole((MAXLEN, HD)), whole((MAXLEN, HD))],
        out_shape=[
            struct((MAXLEN, width), F32),
            struct((MAXLEN, HD), F32), struct((MAXLEN, HD), F32),
        ],
        compiler_params=params(),
        cost_estimate=cost(GROUP * 10 * 384 * 512 * HD, GROUP * 384 * 512, 2**22),
        name="own_grad",
    )(
        vmem(copied), vmem(masked), hbm(comp_keys), hbm(comp_values), lse, delta, past,
    )

    return (
        grad_queries,
        grad_prompt[:, 0:HD],
        grad_prompt[:, HD:],
        grad_comp_keys,
        grad_comp_values,
    )


def solution(mesh):
    rows = P(("grp", "comp"), "tp")
    return jax.shard_map(
        per_device,
        mesh=mesh,
        in_specs=(rows,) * 6 + (P(("grp", "comp")),),
        out_specs=(rows,) * 5,
        check_vma=False,
    )
```

```python
import jax
import jax.numpy as jnp
from jax import lax
from jax.experimental import pallas as pl
from jax.experimental.pallas import tpu as pltpu
from jax.sharding import PartitionSpec as P

HD = 128
BLK = 128
MAXLEN = 512
GROUP = 5
QB = 256
SHARD = 32
SCALE = HD ** (-0.5)
LOG2E = 1.4426950408889634
C2 = SCALE * LOG2E
F32 = jnp.float32
BF16 = jnp.bfloat16
VMEM_LIMIT = 40 * 1024 * 1024

NT = (((1,), (1,)), ((), ()))


def dot(a, b):
    return jnp.dot(a, b, preferred_element_type=F32)


def dot_nt(a, b):
    return lax.dot_general(a, b, NT, preferred_element_type=F32)


def causal_keep(rows, first_row):
    u = lax.broadcasted_iota(jnp.int32, (rows, QB), 0)
    i = lax.broadcasted_iota(jnp.int32, (rows, QB), 1)
    return u <= i


def lanes(head):
    return pl.ds(pl.multiple_of(head * HD, HD), HD)


def spread_kernel(k_ref, v_ref, out_ref, held_ref, sems):
    copies = [
        pltpu.make_async_copy(src, held_ref.at[i], sems.at[i])
        for i, src in enumerate((k_ref, v_ref))
    ]
    for copy in copies:
        copy.start()
    for copy in copies:
        copy.wait()
    for device in range(out_ref.shape[0]):
        out_ref[device, :, 0:HD] = held_ref[0]
        out_ref[device, :, HD:] = held_ref[1]


def own_stats_kernel(
    len_ref, q_ref, g_ref, k_ref, v_ref, copy_ref, masked_ref, max_ref, sum_ref, del_ref
):
    live = lax.broadcasted_iota(jnp.int32, (MAXLEN, 1), 0) < BLK * len_ref[0]
    g = jnp.where(live, g_ref[...], jnp.zeros((), BF16))
    masked_ref[...] = g
    copy_ref[...] = q_ref[...]
    keep = causal_keep(QB, 0)
    for block in range(MAXLEN // QB):
        lo = block * QB
        hi = lo + QB
        q = q_ref[lo:hi, :]
        gb = g[lo:hi, :]
        diag = jnp.where(keep, dot_nt(k_ref[lo:hi, :], q), -jnp.inf)
        top = jnp.max(diag, axis=0, keepdims=True)
        if block:
            past = dot_nt(k_ref[0:lo, :], q)
            top = jnp.maximum(top, jnp.max(past, axis=0, keepdims=True))
        top = top * C2
        e = jnp.exp2(diag * C2 - top)
        total = jnp.sum(e, axis=0, keepdims=True)
        delta = jnp.sum(e * dot_nt(v_ref[lo:hi, :], gb), axis=0, keepdims=True)
        if block:
            e = jnp.exp2(past * C2 - top)
            total = total + jnp.sum(e, axis=0, keepdims=True)
            delta = delta + jnp.sum(e * dot_nt(v_ref[0:lo, :], gb), axis=0, keepdims=True)
        max_ref[0, :, lo:hi] = top
        sum_ref[0, :, lo:hi] = total
        del_ref[0, :, lo:hi] = delta


def prompt_kernel(
    q_ref, g_ref, kv_ref, max_ref, sum_ref, del_ref,
    dq_ref, grad_ref, lse_ref, delta_ref,
    total_ref, kt_ref, ks_ref, *scratch,
):
    tokens = kv_ref.shape[0]
    tile = 64
    blocks = MAXLEN // QB
    items = GROUP * blocks

    def place(item):
        head, block = divmod(item, blocks)
        return head, slice(block * QB, (block + 1) * QB), slice(head * HD, (head + 1) * HD)

    def buffers(item):
        return scratch[item % 2 * 5 : item % 2 * 5 + 5]

    def scores(item):
        _, rows, cols = place(item)
        s_ref, dp_ref, _, _, top_ref = buffers(item)
        q = q_ref[rows, cols]
        s = dot_nt(ks_ref[...], jnp.concatenate([q, q], axis=1))
        s_ref[...] = s
        top_ref[...] = jnp.max(s.reshape(tokens // 8, 8, QB), axis=0)
        dp_ref[...] = dot_nt(kv_ref[:, HD:], g_ref[rows, cols])

    def softmax(item):
        head, rows, _ = place(item)
        s_ref, dp_ref, p_ref, d_ref, top_ref = buffers(item)
        own_top = max_ref[head, :, rows]
        top = jnp.maximum(jnp.max(top_ref[...], axis=0, keepdims=True), own_top)
        own = jnp.exp2(own_top - top)
        total = jnp.zeros((8, QB), F32)
        delta = jnp.zeros((8, QB), F32)
        for t in range(0, tokens, tile):
            e = jnp.exp2(s_ref[t : t + tile, :] - top)
            s_ref[t : t + tile, :] = e
            total = total + jnp.sum(e.reshape(tile // 8, 8, QB), axis=0)
            ed = e * dp_ref[t : t + tile, :]
            delta = delta + jnp.sum(ed.reshape(tile // 8, 8, QB), axis=0)
        total = jnp.sum(total, axis=0, keepdims=True) + own * sum_ref[head, :, rows]
        delta = jnp.sum(delta, axis=0, keepdims=True) + own * del_ref[head, :, rows]
        inverse = 1.0 / total
        delta = delta * inverse
        lse_ref[head, :, rows] = top + jnp.log2(total)
        delta_ref[head, :, rows] = delta
        for t in range(0, tokens, tile):
            p = s_ref[t : t + tile, :] * inverse
            p_ref[t : t + tile, :] = p.astype(BF16)
            d_ref[t : t + tile, :] = (p * (dp_ref[t : t + tile, :] - delta)).astype(BF16)

    def grads(item):
        head, rows, cols = place(item)
        _, _, p_ref, d_ref, _ = buffers(item)
        total_ref[:, HD:] += dot(p_ref[...], g_ref[rows, cols])
        total_ref[:, 0:HD] += dot(d_ref[...], q_ref[rows, cols])
        dq_ref[head, :, rows] = dot(kt_ref[...], d_ref[...])

    keys = kv_ref[:, 0:HD]
    kt_ref[...] = keys.T
    scaled = keys.astype(F32) * C2
    high = scaled.astype(BF16)
    ks_ref[:, 0:HD] = high
    ks_ref[:, HD:] = (scaled - high.astype(F32)).astype(BF16)
    total_ref[...] = jnp.zeros_like(total_ref)

    for step in range(-1, items + 1):
        if step + 1 < items:
            scores(step + 1)
        if 0 <= step < items:
            softmax(step)
        if step >= 1:
            grads(step - 1)

    grad_ref[:, 0:HD] = (total_ref[:, 0:HD] * SCALE).astype(BF16)
    grad_ref[:, HD:] = total_ref[:, HD:].astype(BF16)


def own_grad_kernel(
    q_ref, g_ref, k_ref, v_ref, lse_ref, delta_ref, past_ref, dq_ref, dk_ref, dv_ref
):
    head = pl.program_id(0)

    @pl.when(head == 0)
    def _():
        dk_ref[...] = jnp.zeros_like(dk_ref)
        dv_ref[...] = jnp.zeros_like(dv_ref)

    keep = causal_keep(QB, 0)
    keys_t = k_ref[...].T
    for block in range(MAXLEN // QB):
        lo = block * QB
        hi = lo + QB
        q = q_ref[lo:hi, lanes(head)]
        gb = g_ref[lo:hi, lanes(head)]
        lse = lse_ref[head, :, lo:hi]
        delta = delta_ref[head, :, lo:hi]
        p = jnp.exp2(dot_nt(k_ref[0:hi, :], q) * C2 - lse)
        last = jnp.where(keep, p[lo:hi], 0.0)
        p = jnp.concatenate([p[0:lo], last], axis=0) if block else last
        ds = (p * (dot_nt(v_ref[0:hi, :], gb) - delta)).astype(BF16)
        dv_ref[0:hi, :] += dot(p.astype(BF16), gb)
        dk_ref[0:hi, :] += dot(ds, q)
        part = past_ref[head, :, lo:hi] + dot(keys_t[:, 0:hi], ds)
        dq_ref[lo:hi, :] = part.T * SCALE

    @pl.when(head == GROUP - 1)
    def _():
        dk_ref[...] = dk_ref[...] * SCALE


def whole(shape):
    return pl.BlockSpec(shape, lambda h: (0,) * len(shape))


HEAD = pl.BlockSpec((MAXLEN, HD), lambda h: (0, h))
ROW = pl.BlockSpec((1, 1, MAXLEN), lambda h: (h, 0, 0))


def params():
    return pltpu.CompilerParams(
        dimension_semantics=("arbitrary",), vmem_limit_bytes=VMEM_LIMIT
    )


def cost(flops, exps, moved):
    return pl.CostEstimate(flops=flops, transcendentals=exps, bytes_accessed=moved)


def struct(shape, dtype):
    return jax.ShapeDtypeStruct(shape, dtype)


def vmem_struct(shape, dtype):
    return pltpu.VMEM(shape, dtype)


def vmem(x):
    return pltpu.with_memory_space_constraint(x, pltpu.VMEM)


def hbm(x):
    return pltpu.with_memory_space_constraint(x, pltpu.HBM)


SMEM = pl.BlockSpec(memory_space=pltpu.SMEM)
VMEM = pl.BlockSpec(memory_space=pltpu.VMEM)


def per_device(queries, comp_keys, comp_values, out_grad, prompt_keys, prompt_values, lengths):
    devices = lax.axis_size("comp")
    tokens = devices * SHARD
    width = GROUP * HD

    spread = pl.pallas_call(
        spread_kernel,
        in_specs=[pl.BlockSpec(memory_space=pltpu.HBM)] * 2,
        out_specs=VMEM,
        out_shape=struct((devices, SHARD, 2 * HD), BF16),
        scratch_shapes=[pltpu.VMEM((2, SHARD, HD), BF16), pltpu.SemaphoreType.DMA((2,))],
        name="spread",
    )(prompt_keys, prompt_values)
    prompt = lax.all_to_all(spread, "comp", 0, 0, tiled=True)

    stat = struct((GROUP, 1, MAXLEN), F32)
    copied, masked, own_max, own_sum, own_del = pl.pallas_call(
        own_stats_kernel,
        grid=(GROUP,),
        in_specs=[SMEM, HEAD, HEAD, whole((MAXLEN, HD)), whole((MAXLEN, HD))],
        out_specs=[HEAD, HEAD, ROW, ROW, ROW],
        out_shape=[
            vmem_struct((MAXLEN, width), BF16), vmem_struct((MAXLEN, width), BF16),
            stat, stat, stat,
        ],
        compiler_params=params(),
        cost_estimate=cost(GROUP * 4 * 384 * 512 * HD, GROUP * 384 * 512, 2**21),
        name="own_stats",
    )(lengths, hbm(queries), hbm(out_grad), hbm(comp_keys), hbm(comp_values))

    prompt, masked = lax.optimization_barrier((prompt, masked))

    past, grad_part, lse, delta = pl.pallas_call(
        prompt_kernel,
        in_specs=[VMEM] * 6,
        out_specs=[VMEM] * 4,
        out_shape=[
            struct((GROUP, HD, MAXLEN), F32), struct((tokens, 2 * HD), BF16), stat, stat,
        ],
        scratch_shapes=[
            pltpu.VMEM((tokens, 2 * HD), F32),
            pltpu.VMEM((HD, tokens), BF16),
            pltpu.VMEM((tokens, 2 * HD), BF16),
        ]
        + [
            pltpu.VMEM((tokens, QB), F32),
            pltpu.VMEM((tokens, QB), F32),
            pltpu.VMEM((tokens, QB), BF16),
            pltpu.VMEM((tokens, QB), BF16),
            pltpu.VMEM((8, QB), F32),
        ]
        * 2,
        compiler_params=pltpu.CompilerParams(vmem_limit_bytes=VMEM_LIMIT),
        cost_estimate=cost(GROUP * 10 * 1024 * 512 * HD, GROUP * 1024 * 512, 2**22),
        name="prompt",
    )(
        vmem(copied), vmem(masked), prompt.reshape(tokens, 2 * HD), own_max, own_sum, own_del,
    )

    parts = grad_part.reshape(devices, SHARD, 2 * HD)
    arrived = lax.all_to_all(parts, "comp", 0, 0, tiled=True)
    grad_prompt = jnp.sum(arrived.astype(F32), axis=0)

    grad_queries, grad_comp_keys, grad_comp_values = pl.pallas_call(
        own_grad_kernel,
        grid=(GROUP,),
        in_specs=[VMEM, VMEM, whole((MAXLEN, HD)), whole((MAXLEN, HD)), VMEM, VMEM, VMEM],
        out_specs=[HEAD, whole((MAXLEN, HD)), whole((MAXLEN, HD))],
        out_shape=[
            struct((MAXLEN, width), F32),
            struct((MAXLEN, HD), F32), struct((MAXLEN, HD), F32),
        ],
        compiler_params=params(),
        cost_estimate=cost(GROUP * 10 * 384 * 512 * HD, GROUP * 384 * 512, 2**22),
        name="own_grad",
    )(
        vmem(copied), vmem(masked), hbm(comp_keys), hbm(comp_values), lse, delta, past,
    )

    return (
        grad_queries,
        grad_prompt[:, 0:HD],
        grad_prompt[:, HD:],
        grad_comp_keys,
        grad_comp_values,
    )


def solution(mesh):
    rows = P(("grp", "comp"), "tp")
    return jax.shard_map(
        per_device,
        mesh=mesh,
        in_specs=(rows,) * 6 + (P(("grp", "comp")),),
        out_specs=(rows,) * 5,
        check_vma=False,
    )
```

```python
import jax
import jax.numpy as jnp
from jax import lax
from jax.experimental import pallas as pl
from jax.experimental.pallas import tpu as pltpu
from jax.sharding import PartitionSpec as P

HD = 128
BLK = 128
MAXLEN = 512
GROUP = 5
QB = 256
SHARD = 32
SCALE = HD ** (-0.5)
LOG2E = 1.4426950408889634
C2 = SCALE * LOG2E
F32 = jnp.float32
BF16 = jnp.bfloat16
VMEM_LIMIT = 40 * 1024 * 1024

NT = (((1,), (1,)), ((), ()))


def dot(a, b):
    return jnp.dot(a, b, preferred_element_type=F32)


def dot_nt(a, b):
    return lax.dot_general(a, b, NT, preferred_element_type=F32)


def causal_keep(rows, first_row):
    u = lax.broadcasted_iota(jnp.int32, (rows, QB), 0)
    i = lax.broadcasted_iota(jnp.int32, (rows, QB), 1)
    return u <= i


def lanes(head):
    return pl.ds(pl.multiple_of(head * HD, HD), HD)


def spread_kernel(k_ref, v_ref, out_ref, held_ref, sems):
    copies = [
        pltpu.make_async_copy(src, held_ref.at[i], sems.at[i])
        for i, src in enumerate((k_ref, v_ref))
    ]
    for copy in copies:
        copy.start()
    for copy in copies:
        copy.wait()
    for chip in range(out_ref.shape[0]):
        out_ref[chip, :, 0:HD] = held_ref[0]
        out_ref[chip, :, HD:] = held_ref[1]


def own_stats_kernel(
    len_ref, q_ref, g_ref, k_ref, v_ref, copy_ref, masked_ref, max_ref, sum_ref, del_ref
):
    live = lax.broadcasted_iota(jnp.int32, (MAXLEN, 1), 0) < BLK * len_ref[0]
    g = jnp.where(live, g_ref[...], jnp.zeros((), BF16))
    masked_ref[...] = g
    copy_ref[...] = q_ref[...]
    keep = causal_keep(QB, 0)
    for block in range(MAXLEN // QB):
        lo = block * QB
        hi = lo + QB
        q = q_ref[lo:hi, :]
        gb = g[lo:hi, :]
        diag = jnp.where(keep, dot_nt(k_ref[lo:hi, :], q), -jnp.inf)
        top = jnp.max(diag, axis=0, keepdims=True)
        if block:
            past = dot_nt(k_ref[0:lo, :], q)
            top = jnp.maximum(top, jnp.max(past, axis=0, keepdims=True))
        top = top * C2
        e = jnp.exp2(diag * C2 - top)
        total = jnp.sum(e, axis=0, keepdims=True)
        delta = jnp.sum(e * dot_nt(v_ref[lo:hi, :], gb), axis=0, keepdims=True)
        if block:
            e = jnp.exp2(past * C2 - top)
            total = total + jnp.sum(e, axis=0, keepdims=True)
            delta = delta + jnp.sum(e * dot_nt(v_ref[0:lo, :], gb), axis=0, keepdims=True)
        max_ref[0, :, lo:hi] = top
        sum_ref[0, :, lo:hi] = total
        del_ref[0, :, lo:hi] = delta


def prompt_kernel(
    q_ref, g_ref, mine_ref, other_ref, max_ref, sum_ref, del_ref,
    ds_ref, keep_ref, send_ref, lse_ref, delta_ref,
    total_ref, ks_ref, v_ref, d_ref, prob_ref, sems, *scratch,
):
    half = mine_ref.shape[0]
    tokens = 2 * half
    tile = 64
    blocks = MAXLEN // QB
    items = GROUP * blocks

    def place(item):
        head, block = divmod(item, blocks)
        return head, slice(block * QB, (block + 1) * QB), slice(head * HD, (head + 1) * HD)

    def buffers(item):
        return scratch[item % 2 * 3 : item % 2 * 3 + 3]

    def scores(item):
        _, rows, cols = place(item)
        s_ref, dp_ref, top_ref = buffers(item)
        q = q_ref[rows, cols]
        s = dot_nt(ks_ref[...], jnp.concatenate([q, q], axis=1))
        s_ref[...] = s
        top_ref[...] = jnp.max(s.reshape(tokens // 8, 8, QB), axis=0)
        dp_ref[...] = dot_nt(v_ref[...], g_ref[rows, cols])

    def softmax(item):
        head, rows, _ = place(item)
        s_ref, dp_ref, top_ref = buffers(item)
        own_top = max_ref[head, :, rows]
        top = jnp.maximum(jnp.max(top_ref[...], axis=0, keepdims=True), own_top)
        own = jnp.exp2(own_top - top)
        total = jnp.zeros((8, QB), F32)
        delta = jnp.zeros((8, QB), F32)
        for t in range(0, tokens, tile):
            e = jnp.exp2(s_ref[t : t + tile, :] - top)
            total = total + jnp.sum(e.reshape(tile // 8, 8, QB), axis=0)
            ed = e * dp_ref[t : t + tile, :]
            delta = delta + jnp.sum(ed.reshape(tile // 8, 8, QB), axis=0)
        total = jnp.sum(total, axis=0, keepdims=True) + own * sum_ref[head, :, rows]
        delta = jnp.sum(delta, axis=0, keepdims=True) + own * del_ref[head, :, rows]
        delta = delta * (1.0 / total)
        lse = top + jnp.log2(total)
        lse_ref[head, :, rows] = lse
        delta_ref[head, :, rows] = delta
        for t in range(0, tokens, tile):
            p = jnp.exp2(s_ref[t : t + tile, :] - lse)
            prob_ref[head % 2, t : t + tile, rows] = p.astype(BF16)
            ds = p * (dp_ref[t : t + tile, :] - delta)
            d_ref[head, t : t + tile, rows] = ds.astype(BF16)

    def save(head):
        return pltpu.make_async_copy(d_ref.at[head], ds_ref.at[head], sems.at[head])

    def grads(head):
        cols = slice(head * HD, (head + 1) * HD)
        dv = dot(prob_ref[head % 2], g_ref[:, cols])
        dk = dot(d_ref[head], q_ref[:, cols])
        if head:
            dv = total_ref[:, HD:] + dv
            dk = total_ref[:, 0:HD] + dk
        if head < GROUP - 1:
            total_ref[:, HD:] = dv
            total_ref[:, 0:HD] = dk
            return
        for part, out in ((slice(0, half), keep_ref), (slice(half, tokens), send_ref)):
            out[:, 0:HD] = (dk[part] * SCALE).astype(out.dtype)
            out[:, HD:] = dv[part].astype(out.dtype)

    for first, side_ref in ((0, mine_ref), (half, other_ref)):
        part = slice(first, first + half)
        v_ref[part, :] = side_ref[:, HD:]
        scaled = side_ref[:, 0:HD].astype(F32) * C2
        high = scaled.astype(BF16)
        ks_ref[part, 0:HD] = high
        ks_ref[part, HD:] = (scaled - high.astype(F32)).astype(BF16)

    scores(0)
    for item in range(items):
        head, block = divmod(item, blocks)
        if item + 1 < items:
            scores(item + 1)
        softmax(item)
        if block == 0 and head:
            grads(head - 1)
        if block == blocks - 1:
            save(head).start()
    grads(GROUP - 1)
    for head in range(GROUP):
        save(head).wait()


def grads_kernel(
    q_ref, g_ref, k_ref, v_ref, lse_ref, delta_ref, mine_ref, other_ref, ds_ref,
    dq_ref, dk_ref, dv_ref, kt_ref,
):
    head = pl.program_id(0)
    half = mine_ref.shape[0]

    @pl.when(head == 0)
    def _():
        kt_ref[:, 0:half] = mine_ref[:, 0:HD].T
        kt_ref[:, half:] = other_ref[:, 0:HD].T
        dk_ref[...] = jnp.zeros_like(dk_ref)
        dv_ref[...] = jnp.zeros_like(dv_ref)

    keep = causal_keep(QB, 0)
    keys_t = k_ref[...].T
    for block in range(MAXLEN // QB):
        lo = block * QB
        hi = lo + QB
        q = q_ref[lo:hi, lanes(head)]
        gb = g_ref[lo:hi, lanes(head)]
        lse = lse_ref[head, :, lo:hi]
        delta = delta_ref[head, :, lo:hi]
        p = jnp.exp2(dot_nt(k_ref[0:hi, :], q) * C2 - lse)
        last = jnp.where(keep, p[lo:hi], 0.0)
        p = jnp.concatenate([p[0:lo], last], axis=0) if block else last
        ds = (p * (dot_nt(v_ref[0:hi, :], gb) - delta)).astype(BF16)
        dv_ref[0:hi, :] += dot(p.astype(BF16), gb)
        dk_ref[0:hi, :] += dot(ds, q)
        part = dot(kt_ref[...], ds_ref[0, :, lo:hi]) + dot(keys_t[:, 0:hi], ds)
        dq_ref[lo:hi, :] = part.T * SCALE

    @pl.when(head == GROUP - 1)
    def _():
        dk_ref[...] = dk_ref[...] * SCALE


def whole(shape):
    return pl.BlockSpec(shape, lambda h: (0,) * len(shape))


HEAD = pl.BlockSpec((MAXLEN, HD), lambda h: (0, h))
ROW = pl.BlockSpec((1, 1, MAXLEN), lambda h: (h, 0, 0))


def params():
    return pltpu.CompilerParams(
        dimension_semantics=("arbitrary",), vmem_limit_bytes=VMEM_LIMIT
    )


def cost(flops, exps, moved):
    return pl.CostEstimate(flops=flops, transcendentals=exps, bytes_accessed=moved)


def struct(shape, dtype):
    return jax.ShapeDtypeStruct(shape, dtype)


def vmem_struct(shape, dtype):
    return pltpu.VMEM(shape, dtype)


def hbm_struct(shape, dtype):
    return pltpu.HBM(shape, dtype)


def vmem(x):
    return pltpu.with_memory_space_constraint(x, pltpu.VMEM)


def hbm(x):
    return pltpu.with_memory_space_constraint(x, pltpu.HBM)


SMEM = pl.BlockSpec(memory_space=pltpu.SMEM)
VMEM = pl.BlockSpec(memory_space=pltpu.VMEM)


def per_device(queries, comp_keys, comp_values, out_grad, prompt_keys, prompt_values, lengths):
    devices = lax.axis_size("comp")
    half = devices * SHARD // 2
    tokens = 2 * half
    width = GROUP * HD

    chips = devices // 2
    swap = [(d, d ^ 1) for d in range(devices)]
    same_core = [[2 * chip + core for chip in range(chips)] for core in range(2)]
    spread = pl.pallas_call(
        spread_kernel,
        in_specs=[pl.BlockSpec(memory_space=pltpu.HBM)] * 2,
        out_specs=VMEM,
        out_shape=struct((chips, SHARD, 2 * HD), BF16),
        scratch_shapes=[pltpu.VMEM((2, SHARD, HD), BF16), pltpu.SemaphoreType.DMA((2,))],
        name="spread",
    )(prompt_keys, prompt_values)
    mine = lax.all_to_all(spread, "comp", 0, 0, axis_index_groups=same_core, tiled=True)
    mine = mine.reshape(half, 2 * HD)

    stat = struct((GROUP, 1, MAXLEN), F32)
    copied, masked, own_max, own_sum, own_del = pl.pallas_call(
        own_stats_kernel,
        grid=(GROUP,),
        in_specs=[SMEM, HEAD, HEAD, whole((MAXLEN, HD)), whole((MAXLEN, HD))],
        out_specs=[HEAD, HEAD, ROW, ROW, ROW],
        out_shape=[
            vmem_struct((MAXLEN, width), BF16), vmem_struct((MAXLEN, width), BF16),
            stat, stat, stat,
        ],
        compiler_params=params(),
        cost_estimate=cost(GROUP * 4 * 384 * 512 * HD, GROUP * 384 * 512, 2**21),
        name="own_stats",
    )(lengths, hbm(queries), hbm(out_grad), hbm(comp_keys), hbm(comp_values))

    mine, masked = lax.optimization_barrier((mine, masked))
    other = lax.ppermute(mine, "comp", swap)

    dscore, grad_keep, grad_send, lse, delta = pl.pallas_call(
        prompt_kernel,
        in_specs=[VMEM] * 7,
        out_specs=[pl.BlockSpec(memory_space=pltpu.HBM)] + [VMEM] * 4,
        out_shape=[
            hbm_struct((GROUP, tokens, MAXLEN), BF16),
            struct((half, 2 * HD), F32), struct((half, 2 * HD), BF16), stat, stat,
        ],
        scratch_shapes=[
            pltpu.VMEM((tokens, 2 * HD), F32),
            pltpu.VMEM((tokens, 2 * HD), BF16),
            pltpu.VMEM((tokens, HD), BF16),
            pltpu.VMEM((GROUP, tokens, MAXLEN), BF16),
            pltpu.VMEM((2, tokens, MAXLEN), BF16),
            pltpu.SemaphoreType.DMA((GROUP,)),
        ]
        + [
            pltpu.VMEM((tokens, QB), F32),
            pltpu.VMEM((tokens, QB), F32),
            pltpu.VMEM((8, QB), F32),
        ]
        * 2,
        compiler_params=pltpu.CompilerParams(vmem_limit_bytes=VMEM_LIMIT),
        cost_estimate=cost(GROUP * 8 * 1024 * 512 * HD, GROUP * 2048 * 512, 2**23),
        name="prompt",
    )(vmem(copied), vmem(masked), mine, other, own_max, own_sum, own_del)

    received = lax.ppermute(grad_send, "comp", swap)
    total = (grad_keep + received.astype(F32)).astype(BF16).reshape(chips, SHARD, 2 * HD)
    arrived = lax.all_to_all(total, "comp", 0, 0, axis_index_groups=same_core, tiled=True)
    grad_prompt = jnp.sum(arrived.astype(F32), axis=0)

    grad_queries, grad_comp_keys, grad_comp_values = pl.pallas_call(
        grads_kernel,
        grid=(GROUP,),
        in_specs=[VMEM, VMEM, whole((MAXLEN, HD)), whole((MAXLEN, HD))]
        + [VMEM] * 4
        + [pl.BlockSpec((1, tokens, MAXLEN), lambda h: (h, 0, 0))],
        out_specs=[HEAD, whole((MAXLEN, HD)), whole((MAXLEN, HD))],
        out_shape=[
            struct((MAXLEN, width), F32),
            struct((MAXLEN, HD), F32), struct((MAXLEN, HD), F32),
        ],
        scratch_shapes=[pltpu.VMEM((HD, tokens), BF16)],
        compiler_params=params(),
        cost_estimate=cost(GROUP * 4 * 1024 * 512 * HD, GROUP * 384 * 512, 2**23),
        name="grads",
    )(
        vmem(copied), vmem(masked), hbm(comp_keys), hbm(comp_values), lse, delta,
        mine, other, hbm(dscore),
    )

    return (
        grad_queries,
        grad_prompt[:, 0:HD],
        grad_prompt[:, HD:],
        grad_comp_keys,
        grad_comp_values,
    )


def solution(mesh):
    rows = P(("grp", "comp"), "tp")
    return jax.shard_map(
        per_device,
        mesh=mesh,
        in_specs=(rows,) * 6 + (P(("grp", "comp")),),
        out_specs=(rows,) * 5,
        check_vma=False,
    )
```

```python
import jax
import jax.numpy as jnp
from jax import lax
from jax.experimental import pallas as pl
from jax.experimental.pallas import tpu as pltpu
from jax.sharding import PartitionSpec as P

HD = 128
BLK = 128
MAXLEN = 512
GROUP = 5
QB = 256
SHARD = 32
SCALE = HD ** (-0.5)
LOG2E = 1.4426950408889634
C2 = SCALE * LOG2E
F32 = jnp.float32
BF16 = jnp.bfloat16
VMEM_LIMIT = 40 * 1024 * 1024

NT = (((1,), (1,)), ((), ()))


def dot(a, b):
    return jnp.dot(a, b, preferred_element_type=F32)


def dot_nt(a, b):
    return lax.dot_general(a, b, NT, preferred_element_type=F32)


def causal_keep(rows, first_row):
    u = lax.broadcasted_iota(jnp.int32, (rows, QB), 0)
    i = lax.broadcasted_iota(jnp.int32, (rows, QB), 1)
    return u <= i


def lanes(head):
    return pl.ds(pl.multiple_of(head * HD, HD), HD)


def spread_kernel(k_ref, v_ref, out_ref, held_ref, sems):
    copies = [
        pltpu.make_async_copy(src, held_ref.at[i], sems.at[i])
        for i, src in enumerate((k_ref, v_ref))
    ]
    for copy in copies:
        copy.start()
    for copy in copies:
        copy.wait()
    for chip in range(out_ref.shape[0]):
        out_ref[chip, :, 0:HD] = held_ref[0]
        out_ref[chip, :, HD:] = held_ref[1]


def own_stats_kernel(
    len_ref, q_ref, g_ref, k_ref, v_ref, copy_ref, masked_ref, max_ref, sum_ref, del_ref
):
    live = lax.broadcasted_iota(jnp.int32, (MAXLEN, 1), 0) < BLK * len_ref[0]
    g = jnp.where(live, g_ref[...], jnp.zeros((), BF16))
    masked_ref[...] = g
    copy_ref[...] = q_ref[...]
    keep = causal_keep(QB, 0)
    for block in range(MAXLEN // QB):
        lo = block * QB
        hi = lo + QB
        q = q_ref[lo:hi, :]
        gb = g[lo:hi, :]
        diag = jnp.where(keep, dot_nt(k_ref[lo:hi, :], q), -jnp.inf)
        top = jnp.max(diag, axis=0, keepdims=True)
        if block:
            past = dot_nt(k_ref[0:lo, :], q)
            top = jnp.maximum(top, jnp.max(past, axis=0, keepdims=True))
        top = top * C2
        e = jnp.exp2(diag * C2 - top)
        total = jnp.sum(e, axis=0, keepdims=True)
        delta = jnp.sum(e * dot_nt(v_ref[lo:hi, :], gb), axis=0, keepdims=True)
        if block:
            e = jnp.exp2(past * C2 - top)
            total = total + jnp.sum(e, axis=0, keepdims=True)
            delta = delta + jnp.sum(e * dot_nt(v_ref[0:lo, :], gb), axis=0, keepdims=True)
        max_ref[0, :, lo:hi] = top
        sum_ref[0, :, lo:hi] = total
        del_ref[0, :, lo:hi] = delta


def prompt_kernel(
    q_ref, g_ref, mine_ref, other_ref, max_ref, sum_ref, del_ref,
    ds_ref, keep_ref, send_ref, lse_ref, delta_ref,
    total_ref, ks_ref, v_ref, d_ref, prob_ref, sems, *scratch,
):
    half = mine_ref.shape[0]
    tokens = 2 * half
    tile = 64
    chunk = tokens // 4
    blocks = MAXLEN // QB
    items = GROUP * blocks

    def place(item):
        head, block = divmod(item, blocks)
        return head, slice(block * QB, (block + 1) * QB), slice(head * HD, (head + 1) * HD)

    def buffers(item):
        return scratch[item % 2 * 3 : item % 2 * 3 + 3]

    def part(c):
        return slice(c * chunk, (c + 1) * chunk)

    def fold(x):
        return x.reshape(x.shape[0] // 8, 8, QB)

    def grad_product(head, c):
        cols = slice(head * HD, (head + 1) * HD)
        if c % 2:
            return dot(prob_ref[head % 2, part(c // 2), :], g_ref[:, cols])
        return dot(d_ref[head, part(c // 2), :], q_ref[:, cols])

    def grad_add(head, c, product):
        lane = slice(HD, 2 * HD) if c % 2 else slice(0, HD)
        if head:
            product = total_ref[part(c // 2), lane] + product
        if head < GROUP - 1:
            total_ref[part(c // 2), lane] = product
            return
        if c % 2 == 0:
            product = product * SCALE
        out = keep_ref if c < 4 else send_ref
        row = c % 4 // 2 * chunk
        out[row : row + chunk, lane] = product.astype(out.dtype)

    def save(head):
        return pltpu.make_async_copy(d_ref.at[head], ds_ref.at[head], sems.at[head])

    def step(item):
        cur = 0 <= item
        ahead = item + 1 < items
        if ahead:
            _, rows_n, cols_n = place(item + 1)
            s_next, dp_next, top_next = buffers(item + 1)
            q = q_ref[rows_n, cols_n]
            q = jnp.concatenate([q, q], axis=1)
            g = g_ref[rows_n, cols_n]
            tops = None
        if cur:
            head, rows, _ = place(item)
            block = item % blocks
            s_ref, dp_ref, top_ref = buffers(item)
            own_top = max_ref[head, :, rows]
            top = jnp.maximum(jnp.max(top_ref[...], axis=0, keepdims=True), own_top)
            own = jnp.exp2(own_top - top)
            total = jnp.zeros((8, QB), F32)
            delta = jnp.zeros((8, QB), F32)
        for c in range(4):
            if ahead:
                s = dot_nt(ks_ref[part(c), :], q)
            if cur:
                for t in range(c * chunk, (c + 1) * chunk, tile):
                    e = jnp.exp2(s_ref[t : t + tile, :] - top)
                    s_ref[t : t + tile, :] = e
                    total = total + jnp.sum(fold(e), axis=0)
                    delta = delta + jnp.sum(fold(e * dp_ref[t : t + tile, :]), axis=0)
            if ahead:
                s_next[part(c), :] = s
                high = jnp.max(fold(s), axis=0)
                tops = high if tops is None else jnp.maximum(tops, high)
        if ahead:
            top_next[...] = tops
        if cur:
            total = jnp.sum(total, axis=0, keepdims=True) + own * sum_ref[head, :, rows]
            delta = jnp.sum(delta, axis=0, keepdims=True) + own * del_ref[head, :, rows]
            inverse = 1.0 / total
            delta = delta * inverse
            lse_ref[head, :, rows] = top + jnp.log2(total)
            delta_ref[head, :, rows] = delta
        for c in range(4):
            if ahead:
                dp = dot_nt(v_ref[part(c), :], g)
            if cur and head:
                product = grad_product(head - 1, 4 * block + c)
            if cur:
                for t in range(c * chunk, (c + 1) * chunk, tile):
                    p = s_ref[t : t + tile, :] * inverse
                    prob_ref[head % 2, t : t + tile, rows] = p.astype(BF16)
                    ds = p * (dp_ref[t : t + tile, :] - delta)
                    d_ref[head, t : t + tile, rows] = ds.astype(BF16)
            if ahead:
                dp_next[part(c), :] = dp
            if cur and head:
                grad_add(head - 1, 4 * block + c, product)

    for first, side_ref in ((0, mine_ref), (half, other_ref)):
        side = slice(first, first + half)
        v_ref[side, :] = side_ref[:, HD:]
        scaled = side_ref[:, 0:HD].astype(F32) * C2
        high = scaled.astype(BF16)
        ks_ref[side, 0:HD] = high
        ks_ref[side, HD:] = (scaled - high.astype(F32)).astype(BF16)

    for item in range(-1, items):
        step(item)
        if item % blocks == blocks - 1 and item >= 0:
            save(item // blocks).start()
    for c in range(8):
        grad_add(GROUP - 1, c, grad_product(GROUP - 1, c))
    for head in range(GROUP):
        save(head).wait()


def grads_kernel(
    q_ref, g_ref, k_ref, v_ref, lse_ref, delta_ref, mine_ref, other_ref, ds_ref,
    dq_ref, dk_ref, dv_ref, kt_ref,
):
    head = pl.program_id(0)
    half = mine_ref.shape[0]

    @pl.when(head == 0)
    def _():
        kt_ref[:, 0:half] = mine_ref[:, 0:HD].T
        kt_ref[:, half:] = other_ref[:, 0:HD].T
        dk_ref[...] = jnp.zeros_like(dk_ref)
        dv_ref[...] = jnp.zeros_like(dv_ref)

    keep = causal_keep(QB, 0)
    keys_t = k_ref[...].T
    for block in range(MAXLEN // QB):
        lo = block * QB
        hi = lo + QB
        q = q_ref[lo:hi, lanes(head)]
        gb = g_ref[lo:hi, lanes(head)]
        lse = lse_ref[head, :, lo:hi]
        delta = delta_ref[head, :, lo:hi]
        p = jnp.exp2(dot_nt(k_ref[0:hi, :], q) * C2 - lse)
        last = jnp.where(keep, p[lo:hi], 0.0)
        p = jnp.concatenate([p[0:lo], last], axis=0) if block else last
        ds = (p * (dot_nt(v_ref[0:hi, :], gb) - delta)).astype(BF16)
        dv_ref[0:hi, :] += dot(p.astype(BF16), gb)
        dk_ref[0:hi, :] += dot(ds, q)
        part = dot(kt_ref[...], ds_ref[0, :, lo:hi]) + dot(keys_t[:, 0:hi], ds)
        dq_ref[lo:hi, :] = part.T * SCALE

    @pl.when(head == GROUP - 1)
    def _():
        dk_ref[...] = dk_ref[...] * SCALE


def whole(shape):
    return pl.BlockSpec(shape, lambda h: (0,) * len(shape))


HEAD = pl.BlockSpec((MAXLEN, HD), lambda h: (0, h))
ROW = pl.BlockSpec((1, 1, MAXLEN), lambda h: (h, 0, 0))


def params():
    return pltpu.CompilerParams(
        dimension_semantics=("arbitrary",), vmem_limit_bytes=VMEM_LIMIT
    )


def cost(flops, exps, moved):
    return pl.CostEstimate(flops=flops, transcendentals=exps, bytes_accessed=moved)


def struct(shape, dtype):
    return jax.ShapeDtypeStruct(shape, dtype)


def vmem_struct(shape, dtype):
    return pltpu.VMEM(shape, dtype)


def hbm_struct(shape, dtype):
    return pltpu.HBM(shape, dtype)


def vmem(x):
    return pltpu.with_memory_space_constraint(x, pltpu.VMEM)


def hbm(x):
    return pltpu.with_memory_space_constraint(x, pltpu.HBM)


SMEM = pl.BlockSpec(memory_space=pltpu.SMEM)
VMEM = pl.BlockSpec(memory_space=pltpu.VMEM)


def per_device(queries, comp_keys, comp_values, out_grad, prompt_keys, prompt_values, lengths):
    devices = lax.axis_size("comp")
    half = devices * SHARD // 2
    tokens = 2 * half
    width = GROUP * HD

    chips = devices // 2
    swap = [(d, d ^ 1) for d in range(devices)]
    same_core = [[2 * chip + core for chip in range(chips)] for core in range(2)]
    spread = pl.pallas_call(
        spread_kernel,
        in_specs=[pl.BlockSpec(memory_space=pltpu.HBM)] * 2,
        out_specs=VMEM,
        out_shape=struct((chips, SHARD, 2 * HD), BF16),
        scratch_shapes=[pltpu.VMEM((2, SHARD, HD), BF16), pltpu.SemaphoreType.DMA((2,))],
        name="spread",
    )(prompt_keys, prompt_values)
    mine = lax.all_to_all(spread, "comp", 0, 0, axis_index_groups=same_core, tiled=True)
    mine = mine.reshape(half, 2 * HD)

    stat = struct((GROUP, 1, MAXLEN), F32)
    copied, masked, own_max, own_sum, own_del = pl.pallas_call(
        own_stats_kernel,
        grid=(GROUP,),
        in_specs=[SMEM, HEAD, HEAD, whole((MAXLEN, HD)), whole((MAXLEN, HD))],
        out_specs=[HEAD, HEAD, ROW, ROW, ROW],
        out_shape=[
            vmem_struct((MAXLEN, width), BF16), vmem_struct((MAXLEN, width), BF16),
            stat, stat, stat,
        ],
        compiler_params=params(),
        cost_estimate=cost(GROUP * 4 * 384 * 512 * HD, GROUP * 384 * 512, 2**21),
        name="own_stats",
    )(lengths, hbm(queries), hbm(out_grad), hbm(comp_keys), hbm(comp_values))

    mine, masked = lax.optimization_barrier((mine, masked))
    other = lax.ppermute(mine, "comp", swap)

    dscore, grad_keep, grad_send, lse, delta = pl.pallas_call(
        prompt_kernel,
        in_specs=[VMEM] * 7,
        out_specs=[pl.BlockSpec(memory_space=pltpu.HBM)] + [VMEM] * 4,
        out_shape=[
            hbm_struct((GROUP, tokens, MAXLEN), BF16),
            struct((half, 2 * HD), F32), struct((half, 2 * HD), BF16), stat, stat,
        ],
        scratch_shapes=[
            pltpu.VMEM((tokens, 2 * HD), F32),
            pltpu.VMEM((tokens, 2 * HD), BF16),
            pltpu.VMEM((tokens, HD), BF16),
            pltpu.VMEM((GROUP, tokens, MAXLEN), BF16),
            pltpu.VMEM((2, tokens, MAXLEN), BF16),
            pltpu.SemaphoreType.DMA((GROUP,)),
        ]
        + [
            pltpu.VMEM((tokens, QB), F32),
            pltpu.VMEM((tokens, QB), F32),
            pltpu.VMEM((8, QB), F32),
        ]
        * 2,
        compiler_params=pltpu.CompilerParams(vmem_limit_bytes=VMEM_LIMIT),
        cost_estimate=cost(GROUP * 8 * 1024 * 512 * HD, GROUP * 2048 * 512, 2**23),
        name="prompt",
    )(vmem(copied), vmem(masked), mine, other, own_max, own_sum, own_del)

    received = lax.ppermute(grad_send, "comp", swap)
    total = (grad_keep + received.astype(F32)).astype(BF16).reshape(chips, SHARD, 2 * HD)
    arrived = lax.all_to_all(total, "comp", 0, 0, axis_index_groups=same_core, tiled=True)
    grad_prompt = jnp.sum(arrived.astype(F32), axis=0)

    grad_queries, grad_comp_keys, grad_comp_values = pl.pallas_call(
        grads_kernel,
        grid=(GROUP,),
        in_specs=[VMEM, VMEM, whole((MAXLEN, HD)), whole((MAXLEN, HD))]
        + [VMEM] * 4
        + [pl.BlockSpec((1, tokens, MAXLEN), lambda h: (h, 0, 0))],
        out_specs=[HEAD, whole((MAXLEN, HD)), whole((MAXLEN, HD))],
        out_shape=[
            struct((MAXLEN, width), F32),
            struct((MAXLEN, HD), F32), struct((MAXLEN, HD), F32),
        ],
        scratch_shapes=[pltpu.VMEM((HD, tokens), BF16)],
        compiler_params=params(),
        cost_estimate=cost(GROUP * 4 * 1024 * 512 * HD, GROUP * 384 * 512, 2**23),
        name="grads",
    )(
        vmem(copied), vmem(masked), hbm(comp_keys), hbm(comp_values), lse, delta,
        mine, other, hbm(dscore),
    )

    return (
        grad_queries,
        grad_prompt[:, 0:HD],
        grad_prompt[:, HD:],
        grad_comp_keys,
        grad_comp_values,
    )


def solution(mesh):
    rows = P(("grp", "comp"), "tp")
    return jax.shard_map(
        per_device,
        mesh=mesh,
        in_specs=(rows,) * 6 + (P(("grp", "comp")),),
        out_specs=(rows,) * 5,
        check_vma=False,
    )
```

```python
import jax
import jax.numpy as jnp
from jax import lax
from jax.experimental import pallas as pl
from jax.experimental.pallas import tpu as pltpu
from jax.sharding import PartitionSpec as P

HD = 128
BLK = 128
MAXLEN = 512
GROUP = 5
QB = 256
SHARD = 32
LATE = 3
SCALE = HD ** (-0.5)
LOG2E = 1.4426950408889634
C2 = SCALE * LOG2E
F32 = jnp.float32
BF16 = jnp.bfloat16
VMEM_LIMIT = 32 * 1024 * 1024

NT = (((1,), (1,)), ((), ()))


def dot(a, b):
    return jnp.dot(a, b, preferred_element_type=F32)


def dot_nt(a, b):
    return lax.dot_general(a, b, NT, preferred_element_type=F32)


def causal_keep(rows, first_row):
    u = lax.broadcasted_iota(jnp.int32, (rows, QB), 0)
    i = lax.broadcasted_iota(jnp.int32, (rows, QB), 1)
    return u <= i


def lanes(head):
    return pl.ds(pl.multiple_of(head * HD, HD), HD)


def own_stats_kernel(
    len_ref, q_ref, g_ref, k_ref, v_ref, copy_ref, masked_ref, max_ref, sum_ref, del_ref
):
    live = lax.broadcasted_iota(jnp.int32, (MAXLEN, 1), 0) < BLK * len_ref[0]
    g = jnp.where(live, g_ref[...], jnp.zeros((), BF16))
    masked_ref[...] = g
    copy_ref[...] = q_ref[...]
    keep = causal_keep(QB, 0)
    for block in range(MAXLEN // QB):
        lo = block * QB
        hi = lo + QB
        q = q_ref[lo:hi, :]
        gb = g[lo:hi, :]
        diag = jnp.where(keep, dot_nt(k_ref[lo:hi, :], q), -jnp.inf)
        top = jnp.max(diag, axis=0, keepdims=True)
        if block:
            past = dot_nt(k_ref[0:lo, :], q)
            top = jnp.maximum(top, jnp.max(past, axis=0, keepdims=True))
        top = top * C2
        e = jnp.exp2(diag * C2 - top)
        total = jnp.sum(e, axis=0, keepdims=True)
        delta = jnp.sum(e * dot_nt(v_ref[lo:hi, :], gb), axis=0, keepdims=True)
        if block:
            e = jnp.exp2(past * C2 - top)
            total = total + jnp.sum(e, axis=0, keepdims=True)
            delta = delta + jnp.sum(e * dot_nt(v_ref[0:lo, :], gb), axis=0, keepdims=True)
        max_ref[0, :, lo:hi] = top
        sum_ref[0, :, lo:hi] = total
        del_ref[0, :, lo:hi] = delta


def prompt_kernel(
    q_ref, g_ref, mine_ref, other_ref, max_ref, sum_ref, del_ref,
    ds_ref, keep_ref, send_ref, lse_ref, delta_ref, late_p_ref, late_d_ref,
    total_ref, ks_ref, v_ref, d_ref, prob_ref, sems, *scratch,
):
    half = mine_ref.shape[0]
    tokens = 2 * half
    tile = 64
    early = GROUP - LATE
    chunk = tokens // 4
    blocks = MAXLEN // QB
    items = GROUP * blocks

    def place(item):
        head, block = divmod(item, blocks)
        return head, slice(block * QB, (block + 1) * QB), slice(head * HD, (head + 1) * HD)

    def buffers(item):
        return scratch[item % 2 * 3 : item % 2 * 3 + 3]

    def part(c):
        return slice(c * chunk, (c + 1) * chunk)

    def fold(x):
        return x.reshape(x.shape[0] // 8, 8, QB)

    def grad_product(head, c):
        cols = slice(head * HD, (head + 1) * HD)
        if c % 2:
            return dot(prob_ref[head % 2, part(c // 2), :], g_ref[:, cols])
        return dot(d_ref[head, part(c // 2), :], q_ref[:, cols])

    def grad_add(head, c, product):
        lane = slice(HD, 2 * HD) if c % 2 else slice(0, HD)
        if head:
            product = total_ref[part(c // 2), lane] + product
        if head < GROUP - 1:
            total_ref[part(c // 2), lane] = product
            return
        if c % 2 == 0:
            product = product * SCALE
        row = c % 4 // 2 * chunk
        send_ref[row : row + chunk, lane] = product.astype(send_ref.dtype)

    def save(head):
        return pltpu.make_async_copy(d_ref.at[head], ds_ref.at[head], sems.at[head])

    def step(item):
        cur = 0 <= item
        ahead = item + 1 < items
        if ahead:
            _, rows_n, cols_n = place(item + 1)
            s_next, dp_next, top_next = buffers(item + 1)
            q = q_ref[rows_n, cols_n]
            q = jnp.concatenate([q, q], axis=1)
            g = g_ref[rows_n, cols_n]
            tops = None
        if cur:
            head, rows, _ = place(item)
            block = item % blocks
            s_ref, dp_ref, top_ref = buffers(item)
            own_top = max_ref[head, :, rows]
            top = jnp.maximum(jnp.max(top_ref[...], axis=0, keepdims=True), own_top)
            own = jnp.exp2(own_top - top)
            total = jnp.zeros((8, QB), F32)
            delta = jnp.zeros((8, QB), F32)
        for c in range(4):
            if ahead:
                s = dot_nt(ks_ref[part(c), :], q)
            if cur:
                for t in range(c * chunk, (c + 1) * chunk, tile):
                    e = jnp.exp2(s_ref[t : t + tile, :] - top)
                    s_ref[t : t + tile, :] = e
                    total = total + jnp.sum(fold(e), axis=0)
                    delta = delta + jnp.sum(fold(e * dp_ref[t : t + tile, :]), axis=0)
            if ahead:
                s_next[part(c), :] = s
                high = jnp.max(fold(s), axis=0)
                tops = high if tops is None else jnp.maximum(tops, high)
        if ahead:
            top_next[...] = tops
        if cur:
            total = jnp.sum(total, axis=0, keepdims=True) + own * sum_ref[head, :, rows]
            delta = jnp.sum(delta, axis=0, keepdims=True) + own * del_ref[head, :, rows]
            inverse = 1.0 / total
            delta = delta * inverse
            lse_ref[head, :, rows] = top + jnp.log2(total)
            delta_ref[head, :, rows] = delta
        for c in range(4):
            if ahead:
                dp = dot_nt(v_ref[part(c), :], g)
            due = cur and head and (block or head - 1 < early)
            if due:
                product = grad_product(head - 1, 4 * block + c)
            if cur:
                for t in range(c * chunk, (c + 1) * chunk, tile):
                    p = s_ref[t : t + tile, :] * inverse
                    ph = p.astype(BF16)
                    ds = (p * (dp_ref[t : t + tile, :] - delta)).astype(BF16)
                    d_ref[head, t : t + tile, rows] = ds
                    if head >= early and t < half:
                        late_p_ref[head - early, t : t + tile, rows] = ph
                        late_d_ref[head - early, t : t + tile, rows] = ds
                    else:
                        prob_ref[head % 2, t : t + tile, rows] = ph
            if ahead:
                dp_next[part(c), :] = dp
            if due:
                grad_add(head - 1, 4 * block + c, product)

    for first, side_ref in ((0, mine_ref), (half, other_ref)):
        side = slice(first, first + half)
        v_ref[side, :] = side_ref[:, HD:]
        scaled = side_ref[:, 0:HD].astype(F32) * C2
        high = scaled.astype(BF16)
        ks_ref[side, 0:HD] = high
        ks_ref[side, HD:] = (scaled - high.astype(F32)).astype(BF16)

    for item in range(-1, items):
        step(item)
        if item % blocks == blocks - 1 and item >= 0:
            save(item // blocks).start()
    for c in range(4, 8):
        grad_add(GROUP - 1, c, grad_product(GROUP - 1, c))
    keep_ref[...] = total_ref[0:half, :]
    for head in range(GROUP):
        save(head).wait()


def keep_kernel(q_ref, g_ref, p_ref, d_ref, early_ref, out_ref):
    dk = early_ref[:, 0:HD]
    dv = early_ref[:, HD:]
    for late in range(LATE):
        head = GROUP - LATE + late
        cols = slice(head * HD, (head + 1) * HD)
        dk = dk + dot(d_ref[late], q_ref[:, cols])
        dv = dv + dot(p_ref[late], g_ref[:, cols])
    out_ref[:, 0:HD] = dk * SCALE
    out_ref[:, HD:] = dv


def grads_kernel(
    q_ref, g_ref, k_ref, v_ref, lse_ref, delta_ref, mine_ref, other_ref, ds_ref,
    dq_ref, dk_ref, dv_ref, kt_ref,
):
    head = pl.program_id(0)
    half = mine_ref.shape[0]

    @pl.when(head == 0)
    def _():
        kt_ref[:, 0:half] = mine_ref[:, 0:HD].T
        kt_ref[:, half:] = other_ref[:, 0:HD].T
        dk_ref[...] = jnp.zeros_like(dk_ref)
        dv_ref[...] = jnp.zeros_like(dv_ref)

    keep = causal_keep(QB, 0)
    keys_t = k_ref[...].T
    for block in range(MAXLEN // QB):
        lo = block * QB
        hi = lo + QB
        q = q_ref[lo:hi, lanes(head)]
        gb = g_ref[lo:hi, lanes(head)]
        lse = lse_ref[head, :, lo:hi]
        delta = delta_ref[head, :, lo:hi]
        p = jnp.exp2(dot_nt(k_ref[0:hi, :], q) * C2 - lse)
        last = jnp.where(keep, p[lo:hi], 0.0)
        p = jnp.concatenate([p[0:lo], last], axis=0) if block else last
        ds = (p * (dot_nt(v_ref[0:hi, :], gb) - delta)).astype(BF16)
        dv_ref[0:hi, :] += dot(p.astype(BF16), gb)
        dk_ref[0:hi, :] += dot(ds, q)
        part = dot(kt_ref[...], ds_ref[0, :, lo:hi]) + dot(keys_t[:, 0:hi], ds)
        dq_ref[lo:hi, :] = part.T * SCALE

    @pl.when(head == GROUP - 1)
    def _():
        dk_ref[...] = dk_ref[...] * SCALE


def whole(shape):
    return pl.BlockSpec(shape, lambda h: (0,) * len(shape))


HEAD = pl.BlockSpec((MAXLEN, HD), lambda h: (0, h))
ROW = pl.BlockSpec((1, 1, MAXLEN), lambda h: (h, 0, 0))


def params():
    return pltpu.CompilerParams(
        dimension_semantics=("arbitrary",), vmem_limit_bytes=VMEM_LIMIT
    )


def cost(flops, exps, moved):
    return pl.CostEstimate(flops=flops, transcendentals=exps, bytes_accessed=moved)


def struct(shape, dtype):
    return jax.ShapeDtypeStruct(shape, dtype)


def vmem_struct(shape, dtype):
    return pltpu.VMEM(shape, dtype)


def hbm_struct(shape, dtype):
    return pltpu.HBM(shape, dtype)


def vmem(x):
    return pltpu.with_memory_space_constraint(x, pltpu.VMEM)


def hbm(x):
    return pltpu.with_memory_space_constraint(x, pltpu.HBM)


SMEM = pl.BlockSpec(memory_space=pltpu.SMEM)
VMEM = pl.BlockSpec(memory_space=pltpu.VMEM)


def per_device(queries, comp_keys, comp_values, out_grad, prompt_keys, prompt_values, lengths):
    devices = lax.axis_size("comp")
    half = devices * SHARD // 2
    tokens = 2 * half
    width = GROUP * HD

    chips = devices // 2
    swap = [(d, d ^ 1) for d in range(devices)]
    same_core = [[2 * chip + core for chip in range(chips)] for core in range(2)]
    side_by_side = jnp.pad(prompt_keys, ((0, 0), (0, HD))) + jnp.pad(
        prompt_values, ((0, 0), (HD, 0))
    )
    spread = jnp.broadcast_to(side_by_side[None], (chips, SHARD, 2 * HD))
    mine = lax.all_to_all(spread, "comp", 0, 0, axis_index_groups=same_core, tiled=True)
    mine = mine.reshape(half, 2 * HD)

    stat = struct((GROUP, 1, MAXLEN), F32)
    copied, masked, own_max, own_sum, own_del = pl.pallas_call(
        own_stats_kernel,
        grid=(GROUP,),
        in_specs=[SMEM, HEAD, HEAD, whole((MAXLEN, HD)), whole((MAXLEN, HD))],
        out_specs=[HEAD, HEAD, ROW, ROW, ROW],
        out_shape=[
            vmem_struct((MAXLEN, width), BF16), vmem_struct((MAXLEN, width), BF16),
            stat, stat, stat,
        ],
        compiler_params=params(),
        cost_estimate=cost(GROUP * 4 * 384 * 512 * HD, GROUP * 384 * 512, 2**21),
        name="own_stats",
    )(lengths, hbm(queries), hbm(out_grad), hbm(comp_keys), hbm(comp_values))

    mine, masked = lax.optimization_barrier((mine, masked))
    other = lax.ppermute(mine, "comp", swap)

    late = (LATE, half, MAXLEN)
    dscore, grad_early, grad_send, lse, delta, late_p, late_d = pl.pallas_call(
        prompt_kernel,
        in_specs=[VMEM] * 7,
        out_specs=[pl.BlockSpec(memory_space=pltpu.HBM)] + [VMEM] * 6,
        out_shape=[
            hbm_struct((GROUP, tokens, MAXLEN), BF16),
            struct((half, 2 * HD), F32), struct((half, 2 * HD), BF16), stat, stat,
            vmem_struct(late, BF16), vmem_struct(late, BF16),
        ],
        scratch_shapes=[
            pltpu.VMEM((tokens, 2 * HD), F32),
            pltpu.VMEM((tokens, 2 * HD), BF16),
            pltpu.VMEM((tokens, HD), BF16),
            pltpu.VMEM((GROUP, tokens, MAXLEN), BF16),
            pltpu.VMEM((2, tokens, MAXLEN), BF16),
            pltpu.SemaphoreType.DMA((GROUP,)),
        ]
        + [
            pltpu.VMEM((tokens, QB), F32),
            pltpu.VMEM((tokens, QB), F32),
            pltpu.VMEM((8, QB), F32),
        ]
        * 2,
        compiler_params=pltpu.CompilerParams(vmem_limit_bytes=VMEM_LIMIT),
        cost_estimate=cost(GROUP * 8 * 1024 * 512 * HD, GROUP * 2048 * 512, 2**23),
        name="prompt",
    )(vmem(copied), vmem(masked), mine, other, own_max, own_sum, own_del)

    received = lax.ppermute(grad_send, "comp", swap)
    grad_keep = pl.pallas_call(
        keep_kernel,
        in_specs=[VMEM] * 5,
        out_specs=VMEM,
        out_shape=struct((half, 2 * HD), F32),
        compiler_params=pltpu.CompilerParams(vmem_limit_bytes=16 * 1024 * 1024),
        cost_estimate=cost(LATE * 2 * 1024 * 512 * HD, 0, 2**22),
        name="keep",
    )(vmem(copied), vmem(masked), vmem(late_p), vmem(late_d), grad_early)
    total = (grad_keep + received.astype(F32)).astype(BF16).reshape(chips, SHARD, 2 * HD)
    arrived = lax.all_to_all(total, "comp", 0, 0, axis_index_groups=same_core, tiled=True)
    grad_prompt = jnp.sum(arrived.astype(F32), axis=0)

    grad_queries, grad_comp_keys, grad_comp_values = pl.pallas_call(
        grads_kernel,
        grid=(GROUP,),
        in_specs=[VMEM, VMEM, whole((MAXLEN, HD)), whole((MAXLEN, HD))]
        + [VMEM] * 4
        + [pl.BlockSpec((1, tokens, MAXLEN), lambda h: (h, 0, 0))],
        out_specs=[HEAD, whole((MAXLEN, HD)), whole((MAXLEN, HD))],
        out_shape=[
            struct((MAXLEN, width), F32),
            struct((MAXLEN, HD), F32), struct((MAXLEN, HD), F32),
        ],
        scratch_shapes=[pltpu.VMEM((HD, tokens), BF16)],
        compiler_params=params(),
        cost_estimate=cost(GROUP * 4 * 1024 * 512 * HD, GROUP * 384 * 512, 2**23),
        name="grads",
    )(
        vmem(copied), vmem(masked), hbm(comp_keys), hbm(comp_values), lse, delta,
        mine, other, hbm(dscore),
    )

    return (
        grad_queries,
        grad_prompt[:, 0:HD],
        grad_prompt[:, HD:],
        grad_comp_keys,
        grad_comp_values,
    )


def solution(mesh):
    rows = P(("grp", "comp"), "tp")
    return jax.shard_map(
        per_device,
        mesh=mesh,
        in_specs=(rows,) * 6 + (P(("grp", "comp")),),
        out_specs=(rows,) * 5,
        check_vma=False,
    )
```

```python
import jax
import jax.numpy as jnp
from jax import lax
from jax.experimental import pallas as pl
from jax.experimental.pallas import tpu as pltpu
from jax.sharding import PartitionSpec as P

HD = 128
BLK = 128
MAXLEN = 512
GROUP = 5
QB = 256
SHARD = 32
LATE = 3
SCALE = HD ** (-0.5)
LOG2E = 1.4426950408889634
C2 = SCALE * LOG2E
F32 = jnp.float32
BF16 = jnp.bfloat16
VMEM_LIMIT = 32 * 1024 * 1024

NT = (((1,), (1,)), ((), ()))


def dot(a, b):
    return jnp.dot(a, b, preferred_element_type=F32)


def dot_nt(a, b):
    return lax.dot_general(a, b, NT, preferred_element_type=F32)


def causal_keep(rows, first_row):
    u = lax.broadcasted_iota(jnp.int32, (rows, QB), 0)
    i = lax.broadcasted_iota(jnp.int32, (rows, QB), 1)
    return u <= i


def lanes(head):
    return pl.ds(pl.multiple_of(head * HD, HD), HD)


def own_stats_kernel(
    len_ref, q_ref, g_ref, k_ref, v_ref, copy_ref, masked_ref, max_ref, sum_ref, del_ref
):
    live = lax.broadcasted_iota(jnp.int32, (MAXLEN, 1), 0) < BLK * len_ref[0]
    g = jnp.where(live, g_ref[...], jnp.zeros((), BF16))
    masked_ref[...] = g
    copy_ref[...] = q_ref[...]
    keep = causal_keep(QB, 0)
    for block in range(MAXLEN // QB):
        lo = block * QB
        hi = lo + QB
        q = q_ref[lo:hi, :]
        gb = g[lo:hi, :]
        diag = jnp.where(keep, dot_nt(k_ref[lo:hi, :], q), -jnp.inf)
        top = jnp.max(diag, axis=0, keepdims=True)
        if block:
            past = dot_nt(k_ref[0:lo, :], q)
            top = jnp.maximum(top, jnp.max(past, axis=0, keepdims=True))
        top = top * C2
        e = jnp.exp2(diag * C2 - top)
        total = jnp.sum(e, axis=0, keepdims=True)
        delta = jnp.sum(e * dot_nt(v_ref[lo:hi, :], gb), axis=0, keepdims=True)
        if block:
            e = jnp.exp2(past * C2 - top)
            total = total + jnp.sum(e, axis=0, keepdims=True)
            delta = delta + jnp.sum(e * dot_nt(v_ref[0:lo, :], gb), axis=0, keepdims=True)
        max_ref[0, :, lo:hi] = top
        sum_ref[0, :, lo:hi] = total
        del_ref[0, :, lo:hi] = delta


def prompt_kernel(
    q_ref, g_ref, mine_ref, other_ref, max_ref, sum_ref, del_ref,
    ds_ref, keep_ref, send_ref, lse_ref, delta_ref, late_p_ref, late_d_ref,
    total_ref, ks_ref, v_ref, vt_ref, d_ref, prob_ref, sems, *scratch,
):
    half = mine_ref.shape[0]
    tokens = 2 * half
    tile = 64
    early = GROUP - LATE
    chunk = tokens // 4
    blocks = MAXLEN // QB
    items = GROUP * blocks

    def place(item):
        head, block = divmod(item, blocks)
        return head, slice(block * QB, (block + 1) * QB), slice(head * HD, (head + 1) * HD)

    def buffers(item):
        return scratch[item % 2 * 2 : item % 2 * 2 + 2]

    def part(c):
        return slice(c * chunk, (c + 1) * chunk)

    def fold(x):
        return x.reshape(x.shape[0] // 8, 8, QB)

    def grad_product(head, c):
        cols = slice(head * HD, (head + 1) * HD)
        if c % 2:
            return dot(prob_ref[head % 2, part(c // 2), :], g_ref[:, cols])
        return dot(d_ref[head, part(c // 2), :], q_ref[:, cols])

    def grad_add(head, c, product):
        lane = slice(HD, 2 * HD) if c % 2 else slice(0, HD)
        if head:
            product = total_ref[part(c // 2), lane] + product
        if head < GROUP - 1:
            total_ref[part(c // 2), lane] = product
            return
        if c % 2 == 0:
            product = product * SCALE
        row = c % 4 // 2 * chunk
        send_ref[row : row + chunk, lane] = product.astype(send_ref.dtype)

    def save(head):
        return pltpu.make_async_copy(d_ref.at[head], ds_ref.at[head], sems.at[head])

    def step(item):
        cur = 0 <= item
        ahead = item + 1 < items
        if ahead:
            _, rows_n, cols_n = place(item + 1)
            s_next, top_next = buffers(item + 1)
            q = q_ref[rows_n, cols_n]
            q = jnp.concatenate([q, q], axis=1)
            tops = None
        if cur:
            head, rows, cols = place(item)
            block = item % blocks
            s_ref, top_ref = buffers(item)
            g = g_ref[rows, cols]
            own_top = max_ref[head, :, rows]
            top = jnp.maximum(jnp.max(top_ref[...], axis=0, keepdims=True), own_top)
            own = jnp.exp2(own_top - top)
            total = jnp.zeros((8, QB), F32)
        for c in range(4):
            if ahead:
                s = dot_nt(ks_ref[part(c), :], q)
            if cur:
                for t in range(c * chunk, (c + 1) * chunk, tile):
                    e = jnp.exp2(s_ref[t : t + tile, :] - top)
                    s_ref[t : t + tile, :] = e
                    total = total + jnp.sum(fold(e), axis=0)
            if ahead:
                s_next[part(c), :] = s
                high = jnp.max(fold(s), axis=0)
                tops = high if tops is None else jnp.maximum(tops, high)
        if ahead:
            top_next[...] = tops
        if not cur:
            return
        total = jnp.sum(total, axis=0, keepdims=True) + own * sum_ref[head, :, rows]
        inverse = 1.0 / total
        lse_ref[head, :, rows] = top + jnp.log2(total)
        due = head and (block or head - 1 < early)
        attended = jnp.zeros((HD, QB), F32)
        for c in range(4):
            if due:
                product = grad_product(head - 1, 4 * block + c)
            late = head >= early and c < 2
            prob, slot = (late_p_ref, head - early) if late else (prob_ref, head % 2)
            for t in range(c * chunk, (c + 1) * chunk, tile):
                p = s_ref[t : t + tile, :] * inverse
                prob[slot, t : t + tile, rows] = p.astype(BF16)
            attended = attended + dot(vt_ref[:, part(c)], prob[slot, part(c), rows])
            if due:
                grad_add(head - 1, 4 * block + c, product)
        delta = jnp.sum(attended * g.T.astype(F32), axis=0, keepdims=True)
        delta = delta + own * inverse * del_ref[head, :, rows]
        delta_ref[head, :, rows] = delta
        for c in range(0, tokens, chunk // 2):
            dp = dot_nt(v_ref[c : c + chunk // 2, :], g)
            for t in range(c, c + chunk // 2, tile):
                p = s_ref[t : t + tile, :] * inverse
                ds = (p * (dp[t - c : t - c + tile] - delta)).astype(BF16)
                d_ref[head, t : t + tile, rows] = ds
                if head >= early and t < half:
                    late_d_ref[head - early, t : t + tile, rows] = ds

    for first, side_ref in ((0, mine_ref), (half, other_ref)):
        side = slice(first, first + half)
        v_ref[side, :] = side_ref[:, HD:]
        vt_ref[:, side] = side_ref[:, HD:].T
        scaled = side_ref[:, 0:HD].astype(F32) * C2
        high = scaled.astype(BF16)
        ks_ref[side, 0:HD] = high
        ks_ref[side, HD:] = (scaled - high.astype(F32)).astype(BF16)

    for item in range(-1, items):
        step(item)
        if item % blocks == blocks - 1 and item >= 0:
            save(item // blocks).start()
    for c in range(4, 8):
        grad_add(GROUP - 1, c, grad_product(GROUP - 1, c))
    keep_ref[...] = total_ref[0:half, :]
    for head in range(GROUP):
        save(head).wait()


def keep_kernel(q_ref, g_ref, p_ref, d_ref, early_ref, out_ref):
    dk = early_ref[:, 0:HD]
    dv = early_ref[:, HD:]
    for late in range(LATE):
        head = GROUP - LATE + late
        cols = slice(head * HD, (head + 1) * HD)
        dk = dk + dot(d_ref[late], q_ref[:, cols])
        dv = dv + dot(p_ref[late], g_ref[:, cols])
    out_ref[:, 0:HD] = dk * SCALE
    out_ref[:, HD:] = dv


def grads_kernel(
    q_ref, g_ref, k_ref, v_ref, lse_ref, delta_ref, mine_ref, other_ref, ds_ref,
    dq_ref, dk_ref, dv_ref, kt_ref,
):
    head = pl.program_id(0)
    half = mine_ref.shape[0]

    @pl.when(head == 0)
    def _():
        kt_ref[:, 0:half] = mine_ref[:, 0:HD].T
        kt_ref[:, half:] = other_ref[:, 0:HD].T
        dk_ref[...] = jnp.zeros_like(dk_ref)
        dv_ref[...] = jnp.zeros_like(dv_ref)

    keep = causal_keep(QB, 0)
    keys_t = k_ref[...].T
    for block in range(MAXLEN // QB):
        lo = block * QB
        hi = lo + QB
        q = q_ref[lo:hi, lanes(head)]
        gb = g_ref[lo:hi, lanes(head)]
        lse = lse_ref[head, :, lo:hi]
        delta = delta_ref[head, :, lo:hi]
        p = jnp.exp2(dot_nt(k_ref[0:hi, :], q) * C2 - lse)
        last = jnp.where(keep, p[lo:hi], 0.0)
        p = jnp.concatenate([p[0:lo], last], axis=0) if block else last
        ds = (p * (dot_nt(v_ref[0:hi, :], gb) - delta)).astype(BF16)
        dv_ref[0:hi, :] += dot(p.astype(BF16), gb)
        dk_ref[0:hi, :] += dot(ds, q)
        part = dot(kt_ref[...], ds_ref[0, :, lo:hi]) + dot(keys_t[:, 0:hi], ds)
        dq_ref[lo:hi, :] = part.T * SCALE

    @pl.when(head == GROUP - 1)
    def _():
        dk_ref[...] = dk_ref[...] * SCALE


def whole(shape):
    return pl.BlockSpec(shape, lambda h: (0,) * len(shape))


HEAD = pl.BlockSpec((MAXLEN, HD), lambda h: (0, h))
ROW = pl.BlockSpec((1, 1, MAXLEN), lambda h: (h, 0, 0))


def params():
    return pltpu.CompilerParams(
        dimension_semantics=("arbitrary",), vmem_limit_bytes=VMEM_LIMIT
    )


def cost(flops, exps, moved):
    return pl.CostEstimate(flops=flops, transcendentals=exps, bytes_accessed=moved)


def struct(shape, dtype):
    return jax.ShapeDtypeStruct(shape, dtype)


def vmem_struct(shape, dtype):
    return pltpu.VMEM(shape, dtype)


def hbm_struct(shape, dtype):
    return pltpu.HBM(shape, dtype)


def vmem(x):
    return pltpu.with_memory_space_constraint(x, pltpu.VMEM)


def hbm(x):
    return pltpu.with_memory_space_constraint(x, pltpu.HBM)


SMEM = pl.BlockSpec(memory_space=pltpu.SMEM)
VMEM = pl.BlockSpec(memory_space=pltpu.VMEM)


def per_device(queries, comp_keys, comp_values, out_grad, prompt_keys, prompt_values, lengths):
    devices = lax.axis_size("comp")
    half = devices * SHARD // 2
    tokens = 2 * half
    width = GROUP * HD

    chips = devices // 2
    swap = [(d, d ^ 1) for d in range(devices)]
    same_core = [[2 * chip + core for chip in range(chips)] for core in range(2)]
    side_by_side = jnp.pad(prompt_keys, ((0, 0), (0, HD))) + jnp.pad(
        prompt_values, ((0, 0), (HD, 0))
    )
    spread = jnp.broadcast_to(side_by_side[None], (chips, SHARD, 2 * HD))
    mine = lax.all_to_all(spread, "comp", 0, 0, axis_index_groups=same_core, tiled=True)
    mine = mine.reshape(half, 2 * HD)

    stat = struct((GROUP, 1, MAXLEN), F32)
    copied, masked, own_max, own_sum, own_del = pl.pallas_call(
        own_stats_kernel,
        grid=(GROUP,),
        in_specs=[SMEM, HEAD, HEAD, whole((MAXLEN, HD)), whole((MAXLEN, HD))],
        out_specs=[HEAD, HEAD, ROW, ROW, ROW],
        out_shape=[
            vmem_struct((MAXLEN, width), BF16), vmem_struct((MAXLEN, width), BF16),
            stat, stat, stat,
        ],
        compiler_params=params(),
        cost_estimate=cost(GROUP * 4 * 384 * 512 * HD, GROUP * 384 * 512, 2**21),
        name="own_stats",
    )(lengths, hbm(queries), hbm(out_grad), hbm(comp_keys), hbm(comp_values))

    mine, masked = lax.optimization_barrier((mine, masked))
    other = lax.ppermute(mine, "comp", swap)

    late = (LATE, half, MAXLEN)
    dscore, grad_early, grad_send, lse, delta, late_p, late_d = pl.pallas_call(
        prompt_kernel,
        in_specs=[VMEM] * 7,
        out_specs=[pl.BlockSpec(memory_space=pltpu.HBM)] + [VMEM] * 6,
        out_shape=[
            hbm_struct((GROUP, tokens, MAXLEN), BF16),
            struct((half, 2 * HD), F32), struct((half, 2 * HD), BF16), stat, stat,
            vmem_struct(late, BF16), vmem_struct(late, BF16),
        ],
        scratch_shapes=[
            pltpu.VMEM((tokens, 2 * HD), F32),
            pltpu.VMEM((tokens, 2 * HD), BF16),
            pltpu.VMEM((tokens, HD), BF16),
            pltpu.VMEM((HD, tokens), BF16),
            pltpu.VMEM((GROUP, tokens, MAXLEN), BF16),
            pltpu.VMEM((2, tokens, MAXLEN), BF16),
            pltpu.SemaphoreType.DMA((GROUP,)),
        ]
        + [
            pltpu.VMEM((tokens, QB), F32),
            pltpu.VMEM((8, QB), F32),
        ]
        * 2,
        compiler_params=pltpu.CompilerParams(vmem_limit_bytes=VMEM_LIMIT),
        cost_estimate=cost(GROUP * 8 * 1024 * 512 * HD, GROUP * 2048 * 512, 2**23),
        name="prompt",
    )(vmem(copied), vmem(masked), mine, other, own_max, own_sum, own_del)

    received = lax.ppermute(grad_send, "comp", swap)
    grad_keep = pl.pallas_call(
        keep_kernel,
        in_specs=[VMEM] * 5,
        out_specs=VMEM,
        out_shape=struct((half, 2 * HD), F32),
        compiler_params=pltpu.CompilerParams(vmem_limit_bytes=16 * 1024 * 1024),
        cost_estimate=cost(LATE * 2 * 1024 * 512 * HD, 0, 2**22),
        name="keep",
    )(vmem(copied), vmem(masked), vmem(late_p), vmem(late_d), grad_early)
    total = (grad_keep + received.astype(F32)).astype(BF16).reshape(chips, SHARD, 2 * HD)
    arrived = lax.all_to_all(total, "comp", 0, 0, axis_index_groups=same_core, tiled=True)
    grad_prompt = jnp.sum(arrived.astype(F32), axis=0)

    grad_queries, grad_comp_keys, grad_comp_values = pl.pallas_call(
        grads_kernel,
        grid=(GROUP,),
        in_specs=[VMEM, VMEM, whole((MAXLEN, HD)), whole((MAXLEN, HD))]
        + [VMEM] * 4
        + [pl.BlockSpec((1, tokens, MAXLEN), lambda h: (h, 0, 0))],
        out_specs=[HEAD, whole((MAXLEN, HD)), whole((MAXLEN, HD))],
        out_shape=[
            struct((MAXLEN, width), F32),
            struct((MAXLEN, HD), F32), struct((MAXLEN, HD), F32),
        ],
        scratch_shapes=[pltpu.VMEM((HD, tokens), BF16)],
        compiler_params=params(),
        cost_estimate=cost(GROUP * 4 * 1024 * 512 * HD, GROUP * 384 * 512, 2**23),
        name="grads",
    )(
        vmem(copied), vmem(masked), hbm(comp_keys), hbm(comp_values), lse, delta,
        mine, other, hbm(dscore),
    )

    return (
        grad_queries,
        grad_prompt[:, 0:HD],
        grad_prompt[:, HD:],
        grad_comp_keys,
        grad_comp_values,
    )


def solution(mesh):
    rows = P(("grp", "comp"), "tp")
    return jax.shard_map(
        per_device,
        mesh=mesh,
        in_specs=(rows,) * 6 + (P(("grp", "comp")),),
        out_specs=(rows,) * 5,
        check_vma=False,
    )
```

```python
import jax
import jax.numpy as jnp
from jax import lax
from jax.experimental import pallas as pl
from jax.experimental.pallas import tpu as pltpu
from jax.sharding import PartitionSpec as P

HD = 128
BLK = 128
MAXLEN = 512
GROUP = 5
QB = 256
SHARD = 32
LATE = 3
SCALE = HD ** (-0.5)
LOG2E = 1.4426950408889634
C2 = SCALE * LOG2E
F32 = jnp.float32
BF16 = jnp.bfloat16
VMEM_LIMIT = 32 * 1024 * 1024

NT = (((1,), (1,)), ((), ()))


def dot(a, b):
    return jnp.dot(a, b, preferred_element_type=F32)


def dot_nt(a, b):
    return lax.dot_general(a, b, NT, preferred_element_type=F32)


def causal_keep(rows, first_row):
    u = lax.broadcasted_iota(jnp.int32, (rows, QB), 0)
    i = lax.broadcasted_iota(jnp.int32, (rows, QB), 1)
    return u <= i


def lanes(head):
    return pl.ds(pl.multiple_of(head * HD, HD), HD)


def spread_kernel(k_ref, v_ref, out_ref, sems):
    copies = [
        pltpu.make_async_copy(
            src, out_ref.at[chip, :, pl.ds(i * HD, HD)], sems.at[2 * chip + i]
        )
        for chip in range(out_ref.shape[0])
        for i, src in enumerate((k_ref, v_ref))
    ]
    for copy in copies:
        copy.start()
    for copy in copies:
        copy.wait()


def own_stats_kernel(
    len_ref, q_ref, g_ref, k_ref, v_ref, copy_ref, masked_ref, max_ref, sum_ref, del_ref
):
    live = lax.broadcasted_iota(jnp.int32, (MAXLEN, 1), 0) < BLK * len_ref[0]
    g = jnp.where(live, g_ref[...], jnp.zeros((), BF16))
    masked_ref[...] = g
    copy_ref[...] = q_ref[...]
    keep = causal_keep(QB, 0)
    for block in range(MAXLEN // QB):
        lo = block * QB
        hi = lo + QB
        q = q_ref[lo:hi, :]
        gb = g[lo:hi, :]
        diag = jnp.where(keep, dot_nt(k_ref[lo:hi, :], q), -jnp.inf)
        top = jnp.max(diag, axis=0, keepdims=True)
        if block:
            past = dot_nt(k_ref[0:lo, :], q)
            top = jnp.maximum(top, jnp.max(past, axis=0, keepdims=True))
        top = top * C2
        e = jnp.exp2(diag * C2 - top)
        total = jnp.sum(e, axis=0, keepdims=True)
        delta = jnp.sum(e * dot_nt(v_ref[lo:hi, :], gb), axis=0, keepdims=True)
        if block:
            e = jnp.exp2(past * C2 - top)
            total = total + jnp.sum(e, axis=0, keepdims=True)
            delta = delta + jnp.sum(e * dot_nt(v_ref[0:lo, :], gb), axis=0, keepdims=True)
        max_ref[0, :, lo:hi] = top
        sum_ref[0, :, lo:hi] = total
        del_ref[0, :, lo:hi] = delta


def prompt_kernel(
    q_ref, g_ref, mine_ref, other_ref, max_ref, sum_ref, del_ref,
    ds_ref, keep_ref, send_ref, lse_ref, delta_ref, late_p_ref, late_d_ref,
    total_ref, ks_ref, v_ref, vt_ref, d_ref, prob_ref, sems, *scratch,
):
    half = mine_ref.shape[0]
    tokens = 2 * half
    tile = 64
    early = GROUP - LATE
    chunk = tokens // 4
    blocks = MAXLEN // QB
    items = GROUP * blocks

    def place(item):
        head, block = divmod(item, blocks)
        return head, slice(block * QB, (block + 1) * QB), slice(head * HD, (head + 1) * HD)

    def buffers(item):
        return scratch[item % 2 * 2 : item % 2 * 2 + 2]

    def part(c):
        return slice(c * chunk, (c + 1) * chunk)

    def fold(x):
        return x.reshape(x.shape[0] // 8, 8, QB)

    def grad_product(head, c):
        cols = slice(head * HD, (head + 1) * HD)
        if c % 2:
            return dot(prob_ref[head % 2, part(c // 2), :], g_ref[:, cols])
        return dot(d_ref[head, part(c // 2), :], q_ref[:, cols])

    def grad_add(head, c, product):
        lane = slice(HD, 2 * HD) if c % 2 else slice(0, HD)
        if head:
            product = total_ref[part(c // 2), lane] + product
        if head < GROUP - 1:
            total_ref[part(c // 2), lane] = product
            return
        if c % 2 == 0:
            product = product * SCALE
        row = c % 4 // 2 * chunk
        send_ref[row : row + chunk, lane] = product.astype(send_ref.dtype)

    def save(head):
        return pltpu.make_async_copy(d_ref.at[head], ds_ref.at[head], sems.at[head])

    def step(item):
        cur = 0 <= item
        ahead = item + 1 < items
        if ahead:
            _, rows_n, cols_n = place(item + 1)
            s_next, top_next = buffers(item + 1)
            q = q_ref[rows_n, cols_n]
            q = jnp.concatenate([q, q], axis=1)
            tops = None
        if cur:
            head, rows, cols = place(item)
            block = item % blocks
            s_ref, top_ref = buffers(item)
            g = g_ref[rows, cols]
            own_top = max_ref[head, :, rows]
            top = jnp.maximum(jnp.max(top_ref[...], axis=0, keepdims=True), own_top)
            own = jnp.exp2(own_top - top)
            total = jnp.zeros((8, QB), F32)
        for c in range(4):
            if ahead:
                s = dot_nt(ks_ref[part(c), :], q)
            if cur:
                for t in range(c * chunk, (c + 1) * chunk, tile):
                    e = jnp.exp2(s_ref[t : t + tile, :] - top)
                    s_ref[t : t + tile, :] = e
                    total = total + jnp.sum(fold(e), axis=0)
            if ahead:
                s_next[part(c), :] = s
                high = jnp.max(fold(s), axis=0)
                tops = high if tops is None else jnp.maximum(tops, high)
        if ahead:
            top_next[...] = tops
        if not cur:
            return
        total = jnp.sum(total, axis=0, keepdims=True) + own * sum_ref[head, :, rows]
        inverse = 1.0 / total
        lse_ref[head, :, rows] = top + jnp.log2(total)
        due = head and (block or head - 1 < early)
        attended = jnp.zeros((HD, QB), F32)
        for c in range(4):
            if due:
                product = grad_product(head - 1, 4 * block + c)
            late = head >= early and c < 2
            prob, slot = (late_p_ref, head - early) if late else (prob_ref, head % 2)
            for t in range(c * chunk, (c + 1) * chunk, tile):
                p = s_ref[t : t + tile, :] * inverse
                prob[slot, t : t + tile, rows] = p.astype(BF16)
            attended = attended + dot(vt_ref[:, part(c)], prob[slot, part(c), rows])
            if due:
                grad_add(head - 1, 4 * block + c, product)
        delta = jnp.sum(attended * g.T.astype(F32), axis=0, keepdims=True)
        delta = delta + own * inverse * del_ref[head, :, rows]
        delta_ref[head, :, rows] = delta
        for c in range(0, tokens, chunk // 2):
            dp = dot_nt(v_ref[c : c + chunk // 2, :], g)
            for t in range(c, c + chunk // 2, tile):
                p = s_ref[t : t + tile, :] * inverse
                ds = (p * (dp[t - c : t - c + tile] - delta)).astype(BF16)
                d_ref[head, t : t + tile, rows] = ds
                if head >= early and t < half:
                    late_d_ref[head - early, t : t + tile, rows] = ds

    for first, side_ref in ((0, mine_ref), (half, other_ref)):
        side = slice(first, first + half)
        v_ref[side, :] = side_ref[:, HD:]
        vt_ref[:, side] = side_ref[:, HD:].T
        scaled = side_ref[:, 0:HD].astype(F32) * C2
        high = scaled.astype(BF16)
        ks_ref[side, 0:HD] = high
        ks_ref[side, HD:] = (scaled - high.astype(F32)).astype(BF16)

    for item in range(-1, items):
        step(item)
        if item % blocks == blocks - 1 and item >= 0:
            save(item // blocks).start()
    for c in range(4, 8):
        grad_add(GROUP - 1, c, grad_product(GROUP - 1, c))
    keep_ref[...] = total_ref[0:half, :]
    for head in range(GROUP):
        save(head).wait()


def keep_kernel(q_ref, g_ref, p_ref, d_ref, early_ref, out_ref):
    dk = early_ref[:, 0:HD]
    dv = early_ref[:, HD:]
    for late in range(LATE):
        head = GROUP - LATE + late
        cols = slice(head * HD, (head + 1) * HD)
        dk = dk + dot(d_ref[late], q_ref[:, cols])
        dv = dv + dot(p_ref[late], g_ref[:, cols])
    out_ref[:, 0:HD] = dk * SCALE
    out_ref[:, HD:] = dv


def grads_kernel(
    q_ref, g_ref, k_ref, v_ref, lse_ref, delta_ref, mine_ref, other_ref, ds_ref,
    dq_ref, dk_ref, dv_ref, kt_ref,
):
    head = pl.program_id(0)
    half = mine_ref.shape[0]

    @pl.when(head == 0)
    def _():
        kt_ref[:, 0:half] = mine_ref[:, 0:HD].T
        kt_ref[:, half:] = other_ref[:, 0:HD].T
        dk_ref[...] = jnp.zeros_like(dk_ref)
        dv_ref[...] = jnp.zeros_like(dv_ref)

    keep = causal_keep(QB, 0)
    keys_t = k_ref[...].T
    for block in range(MAXLEN // QB):
        lo = block * QB
        hi = lo + QB
        q = q_ref[lo:hi, lanes(head)]
        gb = g_ref[lo:hi, lanes(head)]
        lse = lse_ref[head, :, lo:hi]
        delta = delta_ref[head, :, lo:hi]
        p = jnp.exp2(dot_nt(k_ref[0:hi, :], q) * C2 - lse)
        last = jnp.where(keep, p[lo:hi], 0.0)
        p = jnp.concatenate([p[0:lo], last], axis=0) if block else last
        ds = (p * (dot_nt(v_ref[0:hi, :], gb) - delta)).astype(BF16)
        dv_ref[0:hi, :] += dot(p.astype(BF16), gb)
        dk_ref[0:hi, :] += dot(ds, q)
        part = dot(kt_ref[...], ds_ref[0, :, lo:hi]) + dot(keys_t[:, 0:hi], ds)
        dq_ref[lo:hi, :] = part.T * SCALE

    @pl.when(head == GROUP - 1)
    def _():
        dk_ref[...] = dk_ref[...] * SCALE


def whole(shape):
    return pl.BlockSpec(shape, lambda h: (0,) * len(shape))


HEAD = pl.BlockSpec((MAXLEN, HD), lambda h: (0, h))
ROW = pl.BlockSpec((1, 1, MAXLEN), lambda h: (h, 0, 0))


def params():
    return pltpu.CompilerParams(
        dimension_semantics=("arbitrary",), vmem_limit_bytes=VMEM_LIMIT
    )


def cost(flops, exps, moved):
    return pl.CostEstimate(flops=flops, transcendentals=exps, bytes_accessed=moved)


def struct(shape, dtype):
    return jax.ShapeDtypeStruct(shape, dtype)


def vmem_struct(shape, dtype):
    return pltpu.VMEM(shape, dtype)


def hbm_struct(shape, dtype):
    return pltpu.HBM(shape, dtype)


def vmem(x):
    return pltpu.with_memory_space_constraint(x, pltpu.VMEM)


def hbm(x):
    return pltpu.with_memory_space_constraint(x, pltpu.HBM)


SMEM = pl.BlockSpec(memory_space=pltpu.SMEM)
VMEM = pl.BlockSpec(memory_space=pltpu.VMEM)


def per_device(queries, comp_keys, comp_values, out_grad, prompt_keys, prompt_values, lengths):
    devices = lax.axis_size("comp")
    half = devices * SHARD // 2
    tokens = 2 * half
    width = GROUP * HD

    chips = devices // 2
    swap = [(d, d ^ 1) for d in range(devices)]
    same_core = [[2 * chip + core for chip in range(chips)] for core in range(2)]
    spread = pl.pallas_call(
        spread_kernel,
        in_specs=[pl.BlockSpec(memory_space=pltpu.HBM)] * 2,
        out_specs=pl.BlockSpec(memory_space=pltpu.HBM),
        out_shape=hbm_struct((chips, SHARD, 2 * HD), BF16),
        scratch_shapes=[pltpu.SemaphoreType.DMA((2 * chips,))],
        name="spread",
    )(hbm(prompt_keys), hbm(prompt_values))
    mine = lax.all_to_all(spread, "comp", 0, 0, axis_index_groups=same_core, tiled=True)
    mine = mine.reshape(half, 2 * HD)

    stat = struct((GROUP, 1, MAXLEN), F32)
    copied, masked, own_max, own_sum, own_del = pl.pallas_call(
        own_stats_kernel,
        grid=(GROUP,),
        in_specs=[SMEM, HEAD, HEAD, whole((MAXLEN, HD)), whole((MAXLEN, HD))],
        out_specs=[HEAD, HEAD, ROW, ROW, ROW],
        out_shape=[
            vmem_struct((MAXLEN, width), BF16), vmem_struct((MAXLEN, width), BF16),
            stat, stat, stat,
        ],
        compiler_params=params(),
        cost_estimate=cost(GROUP * 4 * 384 * 512 * HD, GROUP * 384 * 512, 2**21),
        name="own_stats",
    )(lengths, hbm(queries), hbm(out_grad), hbm(comp_keys), hbm(comp_values))

    mine, masked = lax.optimization_barrier((mine, masked))
    other = lax.ppermute(mine, "comp", swap)

    late = (LATE, half, MAXLEN)
    dscore, grad_early, grad_send, lse, delta, late_p, late_d = pl.pallas_call(
        prompt_kernel,
        in_specs=[VMEM] * 7,
        out_specs=[pl.BlockSpec(memory_space=pltpu.HBM)] + [VMEM] * 6,
        out_shape=[
            hbm_struct((GROUP, tokens, MAXLEN), BF16),
            struct((half, 2 * HD), F32), struct((half, 2 * HD), BF16), stat, stat,
            vmem_struct(late, BF16), vmem_struct(late, BF16),
        ],
        scratch_shapes=[
            pltpu.VMEM((tokens, 2 * HD), F32),
            pltpu.VMEM((tokens, 2 * HD), BF16),
            pltpu.VMEM((tokens, HD), BF16),
            pltpu.VMEM((HD, tokens), BF16),
            pltpu.VMEM((GROUP, tokens, MAXLEN), BF16),
            pltpu.VMEM((2, tokens, MAXLEN), BF16),
            pltpu.SemaphoreType.DMA((GROUP,)),
        ]
        + [
            pltpu.VMEM((tokens, QB), F32),
            pltpu.VMEM((8, QB), F32),
        ]
        * 2,
        compiler_params=pltpu.CompilerParams(vmem_limit_bytes=VMEM_LIMIT),
        cost_estimate=cost(GROUP * 8 * 1024 * 512 * HD, GROUP * 2048 * 512, 2**23),
        name="prompt",
    )(vmem(copied), vmem(masked), mine, other, own_max, own_sum, own_del)

    received = lax.ppermute(grad_send, "comp", swap)
    grad_keep = pl.pallas_call(
        keep_kernel,
        in_specs=[VMEM] * 5,
        out_specs=VMEM,
        out_shape=struct((half, 2 * HD), F32),
        compiler_params=pltpu.CompilerParams(vmem_limit_bytes=16 * 1024 * 1024),
        cost_estimate=cost(LATE * 2 * 1024 * 512 * HD, 0, 2**22),
        name="keep",
    )(vmem(copied), vmem(masked), vmem(late_p), vmem(late_d), grad_early)
    total = (grad_keep + received.astype(F32)).astype(BF16).reshape(chips, SHARD, 2 * HD)
    arrived = lax.all_to_all(total, "comp", 0, 0, axis_index_groups=same_core, tiled=True)
    grad_prompt = jnp.sum(arrived.astype(F32), axis=0)

    grad_queries, grad_comp_keys, grad_comp_values = pl.pallas_call(
        grads_kernel,
        grid=(GROUP,),
        in_specs=[VMEM, VMEM, whole((MAXLEN, HD)), whole((MAXLEN, HD))]
        + [VMEM] * 4
        + [pl.BlockSpec((1, tokens, MAXLEN), lambda h: (h, 0, 0))],
        out_specs=[HEAD, whole((MAXLEN, HD)), whole((MAXLEN, HD))],
        out_shape=[
            struct((MAXLEN, width), F32),
            struct((MAXLEN, HD), F32), struct((MAXLEN, HD), F32),
        ],
        scratch_shapes=[pltpu.VMEM((HD, tokens), BF16)],
        compiler_params=params(),
        cost_estimate=cost(GROUP * 4 * 1024 * 512 * HD, GROUP * 384 * 512, 2**23),
        name="grads",
    )(
        vmem(copied), vmem(masked), hbm(comp_keys), hbm(comp_values), lse, delta,
        mine, other, hbm(dscore),
    )

    return (
        grad_queries,
        grad_prompt[:, 0:HD],
        grad_prompt[:, HD:],
        grad_comp_keys,
        grad_comp_values,
    )


def solution(mesh):
    rows = P(("grp", "comp"), "tp")
    return jax.shard_map(
        per_device,
        mesh=mesh,
        in_specs=(rows,) * 6 + (P(("grp", "comp")),),
        out_specs=(rows,) * 5,
        check_vma=False,
    )
```
